512 devices in a mesh: tm: 8 (over z), gx: 8 (over y_hi, x), gy: 8 (over y_lo, core).
Axes of the slice: x: 4, y: 8 (y_hi: 2, y_lo: 4; y = y_hi * 4 + y_lo), z: 8, core: 2. Of those that a mesh axis runs over, the one named last changes fastest.
Arguments:
- states: float32 [16, 512, 1024], P('tm', 'gx', 'gy'), may hold values from 0.5 to 1.5
- bed: float32 [512, 1024], P('gx', 'gy'), may hold values from -3 to 3
- background_state: float32 [512, 1024], P('gx', 'gy'), may hold values from 0.5 to 1.5
- ice_mask: int32 [512, 1024], P('gx', 'gy'), may hold values 0 or 1
- flow_rate: float32 [512, 1024], P('gx', 'gy'), may hold values from 0.02 to 0.1
- obs_cell: int32 [16, 8, 8, 512], P('tm', 'gx', 'gy'), may hold values from 0 to 8191
- obs_value: float32 [16, 8, 8, 512], P('tm', 'gx', 'gy'), may hold values from 0.5 to 1.5
Outputs:
- states_out: float32 [16, 512, 1024], P('tm', 'gx', 'gy')
- bed_out: float32 [512, 1024], P('gx', 'gy')
The draws below stay inside these ranges and needn't reach their ends.
All inputs are finite; a program needn't handle non-finite values. No bound on the sum of `ice_mask` on one device may be relied on, other than what follows from the above.
Results may differ from the reference program's by a relative error of at most 0.0001.
Values sent between devices are 32-bit elements; how exact they have to be, the bound alone decides.
A program may use at most 64 MiB of HBM per device.

```python
import math
import jax
import jax.numpy as jnp
from jax import lax

CX = 64
CY = 128
OBS = 512
STEPS = 4
OUTER = 2
SLICES = 16
NX = 512
NY = 1024
N_GX = 8
N_GY = 8


def set_ends(entries, rng, low, top_value):
    longest = entries.shape.index(max(entries.shape))
    spots = []
    for shift in (0, 1):
        where = [jax.random.randint(jax.random.fold_in(rng, axis), (), 0, length) for axis, length in enumerate(entries.shape)]
        where[longest] = (where[longest] + shift) % entries.shape[longest]
        spots.append(tuple(where))
    return entries.at[spots[0]].set(low).at[spots[1]].set(top_value)


def steps_of(own_key, extent, cuts, least, top_value):
    gain, own = 1.0, jax.random.fold_in(own_key, 6)
    for dim, blocks in cuts:
        steps = jnp.exp(jax.random.uniform(jax.random.fold_in(own, dim), (blocks,), jnp.float32, least / len(cuts), top_value / len(cuts)))
        gain = gain * jnp.repeat(steps, extent[dim] // blocks).reshape([-1 if axis == dim else 1 for axis in range(len(extent))])
    return gain


def scatter_about(rng, extent, scale, limit, pieces=(), kind=jnp.bfloat16):
    loudness = steps_of(rng, extent, pieces, -0.22, 0.18) if pieces else 1.0
    drawn = jax.random.normal(rng, extent, jnp.float32) * scale * loudness
    return jnp.minimum(jnp.maximum(drawn, -limit), limit).astype(kind)


def setup_inputs(seed: int = 0) -> dict:
    seeds = jax.random.split(jax.random.key(seed), 8)
    states = jnp.clip(0.5 + 1.0 * jax.random.uniform(seeds[0], (SLICES, NX, NY), jnp.float32) ** steps_of(seeds[0], (SLICES, NX, NY), ((0, 8), (1, 8), (2, 8)), -0.2, 0.2), 0.5, 1.5)
    bed = scatter_about(seeds[1], (NX, NY), 0.5, 3.0, ((0, 8), (1, 8)), jnp.float32)
    background_state = jnp.clip(0.5 + 1.0 * jax.random.uniform(seeds[2], (NX, NY), jnp.float32) ** steps_of(seeds[2], (NX, NY), ((0, 8), (1, 8)), -0.2, 0.2), 0.5, 1.5)
    ice_mask = set_ends((jax.random.randint(seeds[3], (NX, NY), 0, 8) < 7).astype(jnp.int32), jax.random.fold_in(seeds[3], 1), 0, 1)
    flow_rate = jnp.clip(jnp.exp(math.log(0.1) - 1.609438 * jax.random.uniform(seeds[4], (NX, NY), jnp.float32) ** steps_of(seeds[4], (NX, NY), ((0, 8), (1, 8)), -0.2, 0.2)), 0.02, 0.1)
    obs_cell = set_ends(jax.random.randint(seeds[5], (SLICES, N_GX, N_GY, OBS), 0, CX * CY), jax.random.fold_in(seeds[5], 1), 0, (CX * CY) - 1).astype(jnp.int32)
    obs_value = jnp.clip(0.5 + 1.0 * jax.random.uniform(seeds[6], (SLICES, N_GX, N_GY, OBS), jnp.float32) ** steps_of(seeds[6], (SLICES, N_GX, N_GY, OBS), ((0, 8), (1, 8), (2, 8)), -0.2, 0.2), 0.5, 1.5)
    return dict(states=states, bed=bed, background_state=background_state, ice_mask=ice_mask, flow_rate=flow_rate, obs_cell=obs_cell, obs_value=obs_value)


bed_rate = 0.1
state_rate = 0.5

def advance(thick, ground, maskf, rate):
    surface = ground + thick
    open_x = maskf[1:, :] * maskf[:-1, :]
    coef_x = 0.5 * (rate[1:, :] + rate[:-1, :]) * open_x
    mean_x = 0.5 * (thick[1:, :] + thick[:-1, :])
    flux_x = coef_x * mean_x * mean_x * (surface[1:, :] - surface[:-1, :])
    open_y = maskf[:, 1:] * maskf[:, :-1]
    coef_y = 0.5 * (rate[:, 1:] + rate[:, :-1]) * open_y
    mean_y = 0.5 * (thick[:, 1:] + thick[:, :-1])
    flux_y = coef_y * mean_y * mean_y * (surface[:, 1:] - surface[:, :-1])
    change = flux_x[1:, 1:-1] - flux_x[:-1, 1:-1] + (flux_y[1:-1, 1:] - flux_y[1:-1, :-1])
    return thick[1:-1, 1:-1] + change

def model(thick, ground, maskf, rate):
    for step in range(STEPS):
        thick = advance(jnp.pad(thick, 1), jnp.pad(ground, 1), jnp.pad(maskf, 1), jnp.pad(rate, 1))
    return thick

def reference(states, bed, background_state, ice_mask, flow_rate, obs_cell, obs_value):
    maskf = ice_mask.astype(jnp.float32)
    rows_tile = NX // N_GX
    cols_tile = NY // N_GY
    tile_row = (jnp.arange(N_GX, dtype=jnp.int32) * rows_tile)[None, :, None, None]
    tile_col = (jnp.arange(N_GY, dtype=jnp.int32) * cols_tile)[None, None, :, None]
    rows = tile_row + obs_cell // cols_tile
    cols = tile_col + obs_cell % cols_tile
    cell_index = (rows * NY + cols).astype(jnp.int32).reshape(SLICES, -1)
    observed = obs_value.reshape(SLICES, -1)
    bed_prior = bed
    for outer in range(OUTER):
        ground = bed
        final = lax.map(lambda thick: model(thick, ground, maskf, flow_rate), states)
        previous = jnp.concatenate([background_state[None], final[:-1]], axis=0)
        misfit = states - previous
        following = jnp.concatenate([misfit[1:], jnp.zeros_like(misfit[:1])], axis=0)
        predicted = jnp.take_along_axis(final.reshape(SLICES, -1), cell_index, axis=1)
        residual = predicted - observed

        def spread(pair):
            values, index = pair
            return jnp.zeros((NX * NY,), jnp.float32).at[index].add(values)
        forcing = lax.map(spread, (residual, cell_index)).reshape(SLICES, NX, NY) - following

        def pull_one(pair):
            thick, weight = pair
            _, pull = jax.vjp(lambda first, second: model(first, second, maskf, flow_rate), thick, ground)
            return pull(weight)
        grad_states, grad_beds = lax.map(pull_one, (states, forcing))
        bed_grad = lax.optimization_barrier(jnp.sum(grad_beds, axis=0))
        bed = bed - bed_rate * (bed_grad + (bed - bed_prior))
        states = states - state_rate * (misfit + grad_states)
    return (states, bed)
```

```python
import functools

import jax
import jax.numpy as jnp
from jax import lax
from jax.experimental import pallas as pl
from jax.experimental.pallas import tpu as pltpu
from jax.sharding import PartitionSpec as P

STEPS = 4
ROWS, COLS = 64, 128
EDGE = 16
HIGH = ROWS + 2 * EDGE
TALL = HIGH + 8
MID = ROWS + EDGE
BLOCK = 16
BED_RATE = 0.1
STATE_RATE = 0.5
MESH = pl.DeviceIdType.MESH

BED, S0, S1, RATE, N0, N1, V0, V1, BACK = range(9)
FIELDS = 9
STRIP = ((0, 16), (16, 16), (32, 16), (48, 16), (64, 12), (76, 12), (88, 12), (100, 12), (112, 8))
AROUND = tuple((a, b) for a in (-1, 1, 0) for b in (-1, 0, 1) if a or b)
INNER = slice(EDGE, EDGE + ROWS)


def when(cond, act):
    if cond is None:
        act()
    else:
        pl.when(cond)(act)


def rolled(value, shift):
    shift %= COLS
    return value if shift == 0 else pltpu.roll(value, shift, value.ndim - 1)


def lane(shape):
    return lax.broadcasted_iota(jnp.int32, shape, len(shape) - 1)


def ahead(main, side):
    last = lane(main.shape) == COLS - 1
    main, side = rolled(main, -1), rolled(side, -1)
    return jnp.where(last, side, main), jnp.where(last, main, side)


def behind(main, side):
    first = lane(main.shape) == 0
    main, side = rolled(main, 1), rolled(side, 1)
    return jnp.where(first, side, main), jnp.where(first, main, side)


def kernel(
    nt, nx, ny,
    states, bed, background, mask, rate, cells, values,
    states_out, bed_out,
    ff, rate_in, mask_in, cell_in, value_in, left_out, right_out, left_in, right_in,
    nxt, nxt_left, nxt_right, gain, coef, slope, path, final, adj, flux, grad,
    sums, sums_last, fin, fin_last, state1, bed1, nxt1,
    load_sem, send_sem, recv_sem,
):
    t, gx, gy = lax.axis_index("tm"), lax.axis_index("gx"), lax.axis_index("gy")

    loads = [
        pltpu.make_async_copy(src, dst, load_sem.at[i])
        for i, (src, dst) in enumerate((
            (cells, cell_in), (values, value_in), (mask, mask_in), (rate, rate_in),
            (states, ff.at[0, S0:S1 + 1, INNER]), (bed, ff.at[0, BED, INNER]),
            (background, ff.at[0, BACK, INNER]),
        ))
    ]
    for load in loads:
        load.start()

    def near(dt, dx, dy):
        parts = [None if d == 0 else (pos + d >= 0) & (pos + d < size)
                 for d, pos, size in ((dt, t, nt), (dx, gx, nx), (dy, gy, ny))]
        parts = [p for p in parts if p is not None]
        return functools.reduce(jnp.logical_and, parts), (t + dt, gx + dx, gy + dy)

    peers = [near(dt, dx, dy) for dt in (-1, 1, 0) for dx, dy in AROUND]
    peers += [(None, (lax.rem(t + d, nt), gx, gy)) for d in range(1, nt)]
    barrier = pltpu.get_barrier_semaphore()
    expected = jnp.int32(0)
    for cond, target in peers:
        when(cond, functools.partial(pl.semaphore_signal, barrier, inc=1, device_id=target, device_id_type=MESH))
        expected = expected + (1 if cond is None else cond.astype(jnp.int32))

    def clear(cond, *parts):
        def act():
            for ref, index in parts:
                ref[index] = jnp.zeros_like(ref[index])
        pl.when(cond)(act)

    for cond, rows in ((gx == 0, slice(0, EDGE)), (gx == nx - 1, slice(EDGE + ROWS, HIGH))):
        clear(cond, (ff, (0, slice(None), rows)), *((r, (rows,)) for r in (left_in, right_in, nxt, nxt_left, nxt_right)))
    clear(gy == 0, (left_in, ...), (nxt_left, ...))
    clear(gy == ny - 1, (right_in, ...), (nxt_right, ...))
    clear(t == nt - 1, (nxt, ...), (nxt_left, ...), (nxt_right, ...), (nxt1, ...))
    tail = slice(HIGH, TALL)
    for ref, index in ((ff, (slice(None), slice(0, 4), tail)), (path, (Ellipsis, tail, slice(None))),
                       (adj, (Ellipsis, tail, slice(None))), (flux, (Ellipsis, slice(0, 8), slice(None))),
                       (grad, (Ellipsis, slice(0, 8), slice(None)))):
        ref[index] = jnp.zeros_like(ref[index])

    loads[0].wait()
    loads[1].wait()
    obs = cells.shape[-1]
    for j in range(2):
        cell, value = cell_in[j, 0], value_in[j, 0]
        row, col = cell // COLS, cell % COLS
        in_row = (lax.broadcasted_iota(jnp.int32, (ROWS, obs), 0) == row).astype(jnp.float32)
        in_col = (lax.broadcasted_iota(jnp.int32, (COLS, obs), 0) == col).astype(jnp.float32).astype(jnp.bfloat16)
        parts = [in_row.astype(jnp.bfloat16)]
        rest = value
        for _ in range(3):
            part = rest.astype(jnp.bfloat16)
            rest = rest - part.astype(jnp.float32)
            parts.append((in_row * part.astype(jnp.float32)).astype(jnp.bfloat16))
        got = lax.dot_general(jnp.concatenate(parts, axis=0), in_col, (((1,), (1,)), ((), ())),
                              preferred_element_type=jnp.float32)
        ff[0, N0 + j, INNER] = got[:ROWS]
        ff[0, V0 + j, INNER] = (got[3 * ROWS:] + got[2 * ROWS:3 * ROWS]) + got[ROWS:2 * ROWS]
    loads[2].wait()
    loads[3].wait()
    ff[0, RATE, INNER] = jnp.where(mask_in[...] != 0, rate_in[...], 0.0)
    for load in loads[4:]:
        load.wait()

    for r in range(0, ROWS, BLOCK):
        at = lane((BLOCK, COLS))
        to_left = to_right = jnp.zeros((BLOCK, COLS), jnp.float32)
        for f, (start, width) in enumerate(STRIP):
            turned = rolled(ff[0, f, EDGE + r:EDGE + r + BLOCK], start)
            to_left = jnp.where((at >= start) & (at < start + width), turned, to_left)
            low = (start - width) % COLS
            if low + width <= COLS:
                here = (at >= low) & (at < low + width)
            else:
                here = (at >= low) | (at < low + width - COLS)
            to_right = jnp.where(here, turned, to_right)
        left_out[r:r + BLOCK] = to_left
        right_out[r:r + BLOCK] = to_right

    def rows_of(d):
        return {-1: (0, EDGE, EDGE + ROWS), 1: (ROWS - EDGE, EDGE, 0), 0: (0, ROWS, EDGE)}[d]

    copies = []

    def remote(cond_to, target, cond_from, src, dst):
        i = len(copies)
        copy = pltpu.make_async_remote_copy(
            src_ref=src, dst_ref=dst, send_sem=send_sem.at[i], recv_sem=recv_sem.at[i],
            device_id=target, device_id_type=MESH)
        copies.append((copy, cond_to, cond_from))
        return copies[-1]

    halo = []
    for dx, dy in AROUND:
        first, count, land = rows_of(dx)
        to, target = near(0, dx, dy)
        come, _ = near(0, -dx, -dy)
        if dy == 0:
            for fields in (slice(0, 4), slice(4, FIELDS)):
                halo.append(remote(to, target, come,
                                   ff.at[0, fields, EDGE + first:EDGE + first + count],
                                   ff.at[0, fields, land:land + count]))
        else:
            src, dst = (left_out, right_in) if dy < 0 else (right_out, left_in)
            halo.append(remote(to, target, come, src.at[first:first + count], dst.at[land:land + count]))
    for dx, dy in AROUND + ((0, 0),):
        first, count, land = rows_of(dx)
        to, target = near(-1, dx, dy)
        come, _ = near(1, -dx, -dy)
        if dy == 0:
            halo.append(remote(to, target, come, ff.at[0, S0, EDGE + first:EDGE + first + count], nxt.at[land:land + count]))
        else:
            src, dst = (left_out, nxt_right) if dy < 0 else (right_out, nxt_left)
            halo.append(remote(to, target, come, src.at[first:first + count], dst.at[land:land + count]))

    pl.semaphore_wait(barrier, expected)
    for copy, to, _ in halo:
        when(to, copy.start)
    for copy, _, come in halo:
        when(come, copy.wait_recv)

    def unpacked(f, left, right, r):
        start, width = STRIP[f]
        at = lane((BLOCK, COLS))
        from_right = rolled(right[r:r + BLOCK], -start)
        from_left = rolled(left[r:r + BLOCK], -start)
        return jnp.where(at < width, from_right, jnp.where(at >= COLS - width, from_left, 0.0))

    more = (t < nt - 1).astype(jnp.float32)
    for r in range(0, HIGH, BLOCK):
        rows = slice(r, r + BLOCK)
        for f in range(FIELDS):
            ff[1, f, rows] = unpacked(f, left_in, right_in, r)
        for p in range(2):
            following = nxt[rows] if p == 0 else unpacked(S0, nxt_left, nxt_right, r)
            gain[p, 0, rows] = ff[p, N0, rows] + 1.0
            gain[p, 1, rows] = ff[p, N1, rows] + more
            adj[p, 0, rows] = ff[p, V0, rows] + ff[p, S1, rows]
            adj[p, 1, rows] = ff[p, V1, rows] + following

    def slopes(source):
        lo, hi = source[1]
        ref = source[0]
        for r in range(lo, hi, BLOCK):
            rows = slice(r, r + BLOCK)
            main, side = ref(0, rows), ref(1, rows)
            for p, (here, up) in enumerate(zip((main, side), ahead(main, side))):
                slope[1, p, rows] = up - here
                slope[0, p, rows] = ref(p, slice(r + 1, r + 1 + BLOCK)) - here

    for r in range(0, HIGH, BLOCK):
        rows = slice(r, r + BLOCK)
        main, side = ff[0, RATE, rows], ff[1, RATE, rows]

        def mean_rate(a, b):
            return jnp.where(jnp.minimum(a, b) > 0.0, 0.5 * (a + b), 0.0)

        for p, (here, up) in enumerate(zip((main, side), ahead(main, side))):
            coef[1, p, rows] = mean_rate(here, up)
            coef[0, p, rows] = mean_rate(here, ff[p, RATE, r + 1:r + 1 + BLOCK])
    slopes((lambda p, rows: ff[p, BED, rows], (0, HIGH)))

    def faces(thick, r):
        rows = slice(r, r + BLOCK)
        here = [thick(p, rows) for p in range(2)]
        up = [[thick(p, slice(r + 1, r + 1 + BLOCK)) for p in range(2)], ahead(*here)]
        mean = [[0.5 * (here[p] + up[d][p]) for p in range(2)] for d in range(2)]
        step = [[(up[d][p] - here[p]) + slope[d, p, rows] for p in range(2)] for d in range(2)]
        return here, mean, step

    def forward(thick, out, lo, hi):
        for r in range(lo, hi, BLOCK):
            rows = slice(r, r + BLOCK)
            here, mean, step = faces(thick, r)
            f = [[coef[d, p, rows] * mean[d][p] * mean[d][p] * step[d][p] for p in range(2)] for d in range(2)]
            left = behind(*f[1])
            for p in range(2):
                flux[p, :, 8 + r:8 + r + BLOCK] = f[0][p]
                change = (f[0][p] - flux[p, :, 7 + r:7 + r + BLOCK]) + (f[1][p] - left[p])
                out(p, rows, here[p] + change)

    def backward(thick, lo, hi, begin):
        for r in range(lo, hi, BLOCK):
            rows = slice(r, r + BLOCK)
            _, mean, step = faces(thick, r)
            lam = [adj[p, :, rows] for p in range(2)]
            up = [[adj[p, :, r + 1:r + 1 + BLOCK] for p in range(2)], ahead(*lam)]
            keep, give = [[], []], [[], []]
            for d in range(2):
                for p in range(2):
                    q = coef[d, p, rows] * mean[d][p] * (lam[p] - up[d][p])
                    g, e = q * mean[d][p], q * step[d][p]
                    keep[d].append(e - g)
                    give[d].append(e + g)
                    both = g[0] + g[1]
                    spot = slice(8 + r, 8 + r + BLOCK)
                    grad[d, p, spot] = both if begin else grad[d, p, spot] + both
            given = behind(*give[1])
            for p in range(2):
                flux[p, :, 8 + r:8 + r + BLOCK] = give[0][p]
                adj[p, :, rows] = lam[p] + (keep[0][p] + flux[p, :, 7 + r:7 + r + BLOCK]) + (keep[1][p] + given[p])

    def bed_gradient(r, count):
        spot, before = slice(8 + r, 8 + r + count), slice(7 + r, 7 + r + count)
        left = behind(grad[1, 0, spot], grad[1, 1, spot])
        return [(grad[0, p, before] - grad[0, p, spot]) + (left[p] - grad[1, p, spot]) for p in range(2)]

    def at_step(k, start):
        return start if k == 0 else (lambda p, rows: path[k - 1, p, :, rows])

    def run(start, which, lo, hi, weights):
        def store(k):
            def put(p, rows, value):
                if k < STEPS:
                    path[k - 1, p, :, rows] = value
                else:
                    final[which, p, :, rows] = value
                    adj[p, :, rows] = weights(p, rows) * value - adj[p, :, rows]
            return put

        for k in range(STEPS):
            forward(at_step(k, start), store(k + 1), lo, hi)

    def pull(start, lo, hi):
        for k in reversed(range(STEPS)):
            backward(at_step(k, start), lo, hi, k == STEPS - 1)

    def weights(p, rows):
        return gain[p, :, rows]

    def broadcast(buffer):
        out = []
        for d in sorted(range(1, nt), key=lambda d: -min(d, nt - d)):
            out.append((remote(None, (lax.rem(t + d, nt), gx, gy), None, buffer.at[t], buffer.at[t]), d))
        for (copy, _, _), _ in out:
            copy.start()
        return [(copy, buffer.at[lax.rem(t + nt - d, nt)]) for (copy, _, _), d in out]

    def arrived(sent):
        for copy, _ in sent:
            copy.wait_recv()

    before, after = near(-1, 0, 0), near(1, 0, 0)
    lo, hi = (HIGH - MID) // 2, (HIGH + MID) // 2
    at = lane((8, COLS))

    def first(p, rows):
        return ff[p, S0:S1 + 1, rows]

    run(first, 0, 0, HIGH, weights)
    fin_copy = remote(after[0], after[1], before[0], final.at[0, :, 1, lo:hi], fin)
    when(after[0], fin_copy[0].start)
    pull(first, 0, HIGH)
    packed = [jnp.zeros((8, COLS), jnp.float32)] * 2
    for k in range(MID // 8):
        main, side = bed_gradient(lo + 8 * k, 8)
        sums[t, 8 * k:8 * k + 8] = main
        turned = rolled(side, 16 * k)
        slot = 16 * (k % 8)
        here = (at >= slot - 8) & (at < slot + 8) if slot else (at < 8) | (at >= COLS - 8)
        packed[k // 8] = jnp.where(here, turned, packed[k // 8])
    sums[t, MID:MID + 8] = packed[0]
    sums[t, MID + 8:MID + 16] = packed[1]
    sent = broadcast(sums)

    when(before[0], fin_copy[0].wait_recv)
    for r in range(lo, hi, BLOCK):
        rows, short = slice(r, r + BLOCK), slice(r - lo, r - lo + BLOCK)
        for p in range(2):
            begun = jnp.where(t == 0, ff[p, BACK, rows], fin[p, short])
            s0, s1 = ff[p, S0, rows], ff[p, S1, rows]
            state1[p, 0, rows] = s0 - STATE_RATE * ((s0 - begun) + adj[p, 0, rows])
            state1[p, 1, rows] = s1 - STATE_RATE * ((s1 - final[0, p, 0, rows]) + adj[p, 1, rows])
    nxt_copy = remote(before[0], before[1], after[0], state1.at[:, 0, lo:hi], nxt1)
    when(before[0], nxt_copy[0].start)

    arrived(sent)

    def total(ref, rows):
        got = ref[0, rows]
        for i in range(1, nt):
            got = got + ref[i, rows]
        return got

    sides = [total(sums, slice(MID + 8 * i, MID + 8 * i + 8)) for i in range(2)]
    for k in range(MID // 8):
        rows = slice(lo + 8 * k, lo + 8 * k + 8)
        main = total(sums, slice(8 * k, 8 * k + 8))
        side = jnp.where((at < 8) | (at >= COLS - 8), rolled(sides[k // 8], -16 * k), 0.0)
        for p, got in enumerate((main, side)):
            bed1[p, rows] = ff[p, BED, rows] - BED_RATE * got

    bed1[:, hi:hi + 8] = jnp.zeros((2, 8, COLS), jnp.float32)
    state1[:, :, hi:hi + 8] = jnp.zeros((2, 2, 8, COLS), jnp.float32)

    def second(p, rows):
        return state1[p, :, rows]

    slopes((lambda p, rows: bed1[p, rows], (lo, hi)))
    for k in range(STEPS - 1):
        forward(at_step(k, second), lambda p, rows, value, k=k: path.__setitem__((k, p, slice(None), rows), value), lo, hi)
    when(after[0], nxt_copy[0].wait_recv)
    for r in range(lo, hi, BLOCK):
        rows, short = slice(r, r + BLOCK), slice(r - lo, r - lo + BLOCK)
        for p in range(2):
            adj[p, 0, rows] = ff[p, V0, rows] + state1[p, 1, rows]
            adj[p, 1, rows] = ff[p, V1, rows] + nxt1[p, short]

    def last(p, rows, value):
        final[1, p, :, rows] = value
        adj[p, :, rows] = weights(p, rows) * value - adj[p, :, rows]

    forward(at_step(STEPS - 1, second), last, lo, hi)
    fin_last_copy = remote(after[0], after[1], before[0], final.at[1, 0, 1, INNER], fin_last)
    when(after[0], fin_last_copy[0].start)
    pull(second, lo, hi)
    for r in range(EDGE, EDGE + ROWS, BLOCK):
        sums_last[t, r - EDGE:r - EDGE + BLOCK] = bed_gradient(r, BLOCK)[0]
    sent_last = broadcast(sums_last)

    when(before[0], fin_last_copy[0].wait_recv)
    for r in range(0, ROWS, BLOCK):
        rows, short = slice(EDGE + r, EDGE + r + BLOCK), slice(r, r + BLOCK)
        begun = jnp.where(t == 0, ff[0, BACK, rows], fin_last[short])
        s0, s1 = state1[0, 0, rows], state1[0, 1, rows]
        states_out[0, short] = s0 - STATE_RATE * ((s0 - begun) + adj[0, 0, rows])
        states_out[1, short] = s1 - STATE_RATE * ((s1 - final[1, 0, 0, rows]) + adj[0, 1, rows])
    arrived(sent_last)
    for r in range(0, ROWS, BLOCK):
        rows, short = slice(EDGE + r, EDGE + r + BLOCK), slice(r, r + BLOCK)
        now = bed1[0, rows]
        bed_out[short] = now - BED_RATE * (total(sums_last, short) + (now - ff[0, BED, rows]))
    for copy, to, _ in copies:
        when(to, copy.wait_send)


def solution(mesh):
    nt, nx, ny = (mesh.shape[a] for a in ("tm", "gx", "gy"))
    f32 = jnp.float32

    def step(states, bed, background, mask, rate, cells, values):
        obs = cells.shape[-1]
        count = 19 + 2 * (nt - 1) + 3
        vmem = pltpu.VMEM
        return pl.pallas_call(
            functools.partial(kernel, nt, nx, ny),
            out_shape=(jax.ShapeDtypeStruct(states.shape, f32), jax.ShapeDtypeStruct(bed.shape, f32)),
            in_specs=[pl.BlockSpec(memory_space=pl.ANY)] * 7,
            out_specs=(pl.BlockSpec(memory_space=vmem),) * 2,
            scratch_shapes=[
                vmem((2, FIELDS, TALL, COLS), f32),
                vmem((ROWS, COLS), f32), vmem((ROWS, COLS), jnp.int32),
                vmem((2, 1, 1, obs), jnp.int32), vmem((2, 1, 1, obs), f32),
                vmem((ROWS, COLS), f32), vmem((ROWS, COLS), f32),
                vmem((HIGH, COLS), f32), vmem((HIGH, COLS), f32),
                vmem((HIGH, COLS), f32), vmem((HIGH, COLS), f32), vmem((HIGH, COLS), f32),
                vmem((2, 2, HIGH, COLS), f32),
                vmem((2, 2, HIGH, COLS), f32), vmem((2, 2, HIGH, COLS), f32),
                vmem((STEPS - 1, 2, 2, TALL, COLS), f32),
                vmem((2, 2, 2, HIGH, COLS), f32),
                vmem((2, 2, TALL, COLS), f32),
                vmem((2, 2, 8 + HIGH, COLS), f32), vmem((2, 2, 8 + HIGH, COLS), f32),
                vmem((nt, MID + 16, COLS), f32), vmem((nt, ROWS, COLS), f32),
                vmem((2, MID, COLS), f32), vmem((ROWS, COLS), f32),
                vmem((2, 2, HIGH, COLS), f32), vmem((2, HIGH, COLS), f32),
                vmem((2, MID, COLS), f32),
                pltpu.SemaphoreType.DMA((7,)),
                pltpu.SemaphoreType.DMA((count,)), pltpu.SemaphoreType.DMA((count,)),
            ],
            compiler_params=pltpu.CompilerParams(
                collective_id=0, has_side_effects=True, vmem_limit_bytes=32 << 20),
            name="assimilate",
        )(states, bed, background, mask, rate, cells, values)

    return jax.shard_map(
        step,
        mesh=mesh,
        in_specs=(P("tm", "gx", "gy"),) + (P("gx", "gy"),) * 4 + (P("tm", "gx", "gy", None),) * 2,
        out_specs=(P("tm", "gx", "gy"), P("gx", "gy")),
        check_vma=False,
    )
```

```python
import functools

import jax
import jax.numpy as jnp
from jax import lax
from jax.experimental import pallas as pl
from jax.experimental.pallas import tpu as pltpu
from jax.sharding import PartitionSpec as P

STEPS = 4
ROWS, COLS = 64, 128
EDGE = 16
HIGH = ROWS + 2 * EDGE
MID = ROWS + EDGE
END = 2 * EDGE
BLOCK = 16
BED_RATE = 0.1
STATE_RATE = 0.5
MESH = pl.DeviceIdType.MESH

BED, S0, S1, RATE, N0, N1, V0, V1, BACK = range(9)
FIELDS = 9
STRIP = ((0, 16), (16, 16), (32, 16), (48, 16), (64, 12), (76, 12), (88, 12), (100, 12), (112, 8))
CORNERS = ((1, -1), (1, 1), (-1, -1), (-1, 1))
AROUND = ((1, 0), (-1, 0)) + CORNERS + ((0, -1), (0, 1))


def when(cond, act):
    if cond is None:
        act()
    else:
        pl.when(cond)(act)


def span(start, size):
    return pl.ds(pl.multiple_of(start, 8), size)


def rolled(value, shift):
    shift %= COLS
    return value if shift == 0 else pltpu.roll(value, shift, value.ndim - 1)


def lane(shape):
    return lax.broadcasted_iota(jnp.int32, shape, len(shape) - 1)


def ahead(main, side):
    last = lane(main.shape) == COLS - 1
    main, side = rolled(main, -1), rolled(side, -1)
    return jnp.where(last, side, main), jnp.where(last, main, side)


def behind(main, side):
    first = lane(main.shape) == 0
    main, side = rolled(main, 1), rolled(side, 1)
    return jnp.where(first, side, main), jnp.where(first, main, side)


def within(at, start, width):
    start %= COLS
    if start + width <= COLS:
        return (at >= start) & (at < start + width)
    return (at >= start) | (at < start + width - COLS)


def counted(cell, value, rows, skip):
    obs = cell.shape[-1]
    row, col = cell // COLS - skip, cell % COLS
    in_row = (lax.broadcasted_iota(jnp.int32, (rows, obs), 0) == row).astype(jnp.float32)
    in_col = (lax.broadcasted_iota(jnp.int32, (COLS, obs), 0) == col).astype(jnp.float32).astype(jnp.bfloat16)
    parts = [in_row.astype(jnp.bfloat16)]
    rest = value
    for _ in range(3):
        part = rest.astype(jnp.bfloat16)
        rest = rest - part.astype(jnp.float32)
        parts.append((in_row * part.astype(jnp.float32)).astype(jnp.bfloat16))
    got = lax.dot_general(jnp.concatenate(parts, axis=0), in_col, (((1,), (1,)), ((), ())),
                          preferred_element_type=jnp.float32)
    return got[:rows], (got[3 * rows:] + got[2 * rows:3 * rows]) + got[rows:2 * rows]


class Model:
    def __init__(self, rows, field, coef, slope, path, adj, flux, grad, gain, final):
        self.rows, self.field, self.coef, self.slope, self.path = rows, field, coef, slope, path
        self.adj, self.flux, self.grad, self.gain, self.final = adj, flux, grad, gain, final

    def blocks(self):
        return [slice(r, r + BLOCK) for r in range(0, self.rows, BLOCK)]

    def clear_ends(self):
        tail = slice(self.rows, self.rows + 8)
        for ref, index in ((self.field, (Ellipsis, tail, slice(None))), (self.path, (Ellipsis, tail, slice(None))),
                           (self.adj, (Ellipsis, tail, slice(None))), (self.flux, (Ellipsis, slice(0, 8), slice(None))),
                           (self.grad, (Ellipsis, slice(0, 8), slice(None)))):
            ref[index] = jnp.zeros_like(ref[index])

    def coefficients(self):
        def mean_rate(a, b):
            return jnp.where(jnp.minimum(a, b) > 0.0, 0.5 * (a + b), 0.0)

        for rows in self.blocks():
            both = [self.field[p, RATE, rows] for p in range(2)]
            for p, (here, up) in enumerate(zip(both, ahead(*both))):
                self.coef[1, p, rows] = mean_rate(here, up)
                self.coef[0, p, rows] = mean_rate(here, self.field[p, RATE, rows.start + 1:rows.stop + 1])

    def slopes(self):
        for rows in self.blocks():
            both = [self.field[p, BED, rows] for p in range(2)]
            for p, (here, up) in enumerate(zip(both, ahead(*both))):
                self.slope[1, p, rows] = up - here
                self.slope[0, p, rows] = self.field[p, BED, rows.start + 1:rows.stop + 1] - here

    def thick(self, k, p, rows):
        return self.field[p, S0:S1 + 1, rows] if k == 0 else self.path[k - 1, p, :, rows]

    def faces(self, k, rows):
        here = [self.thick(k, p, rows) for p in range(2)]
        up = [[self.thick(k, p, slice(rows.start + 1, rows.stop + 1)) for p in range(2)], ahead(*here)]
        mean = [[0.5 * (here[p] + up[d][p]) for p in range(2)] for d in range(2)]
        step = [[(up[d][p] - here[p]) + self.slope[d, p, rows] for p in range(2)] for d in range(2)]
        return here, mean, step

    def forward(self, k):
        for rows in self.blocks():
            here, mean, step = self.faces(k, rows)
            f = [[self.coef[d, p, rows] * mean[d][p] * mean[d][p] * step[d][p] for p in range(2)] for d in range(2)]
            left = behind(*f[1])
            for p in range(2):
                self.flux[p, :, 8 + rows.start:8 + rows.stop] = f[0][p]
                new = here[p] + ((f[0][p] - self.flux[p, :, 7 + rows.start:7 + rows.stop]) + (f[1][p] - left[p]))
                if k + 1 < STEPS:
                    self.path[k, p, :, rows] = new
                else:
                    self.final[p, :, rows] = new

    def force(self):
        for rows in self.blocks():
            for p in range(2):
                self.adj[p, :, rows] = self.gain[p, :, rows] * self.final[p, :, rows] - self.adj[p, :, rows]

    def backward(self, k):
        for rows in self.blocks():
            _, mean, step = self.faces(k, rows)
            lam = [self.adj[p, :, rows] for p in range(2)]
            up = [[self.adj[p, :, rows.start + 1:rows.stop + 1] for p in range(2)], ahead(*lam)]
            spot = slice(8 + rows.start, 8 + rows.stop)
            keep, give = [[], []], [[], []]
            for d in range(2):
                for p in range(2):
                    q = self.coef[d, p, rows] * mean[d][p] * (lam[p] - up[d][p])
                    g, e = q * mean[d][p], q * step[d][p]
                    keep[d].append(e - g)
                    give[d].append(e + g)
                    both = g[0] + g[1]
                    self.grad[d, p, spot] = both if k == STEPS - 1 else self.grad[d, p, spot] + both
            given = behind(*give[1])
            for p in range(2):
                self.flux[p, :, spot] = give[0][p]
                self.adj[p, :, rows] = (
                    lam[p] + (keep[0][p] + self.flux[p, :, 7 + rows.start:7 + rows.stop]) + (keep[1][p] + given[p]))

    def pull(self):
        for k in reversed(range(STEPS)):
            self.backward(k)

    def bed_gradient(self, r, count):
        spot, before = slice(8 + r, 8 + r + count), slice(7 + r, 7 + r + count)
        left = behind(self.grad[1, 0, spot], self.grad[1, 1, spot])
        return [(self.grad[0, p, before] - self.grad[0, p, spot]) + (left[p] - self.grad[1, p, spot]) for p in range(2)]


def kernel(
    nt, nx, ny,
    states, bed, background, mask, rate, cells, values,
    states_out, bed_out,
    ff, rate_in, mask_in, cell_in, value_in, cell_near, value_near, left_out, right_out, left_in, right_in,
    nxt, fold_out, fold_in, foll1, foll2,
    field1, coef1, slope1, path1, adj1, flux1, grad1, gain1, final1,
    field2, coef2, slope2, path2, adj2, flux2, grad2, gain2, final2,
    field3, gain3, final3, final4,
    pull1, pull2, pull3, back1, back2,
    mine, theirs, pairs, sums2, sums3, sums4, fin_out1, fin_out2, fin1, fin2, fin_last, lam_out1, lam_out2, lam1, lam2,
    load_sem, send_sem, recv_sem,
):
    t, gx, gy = lax.axis_index("tm"), lax.axis_index("gx"), lax.axis_index("gy")
    half = nx // 2
    low = gx < half
    high = jnp.logical_not(low)

    def place(side, is_low):
        return jnp.where(is_low, *{-1: (0, MID), 0: (EDGE, 0), 1: (MID, ROWS)}[side])

    home = place(0, low)
    inner = span(home, ROWS)

    loads = [
        pltpu.make_async_copy(src, dst, load_sem.at[i])
        for i, (src, dst) in enumerate((
            (cells, cell_in), (values, value_in), (mask, mask_in), (rate, rate_in),
            (states, ff.at[S0:S1 + 1, inner]), (bed, ff.at[BED, inner]), (background, ff.at[BACK, inner]),
        ))
    ]
    for load in loads:
        load.start()

    def near(dt, dx, dy):
        parts = [None if d == 0 else (pos + d >= 0) & (pos + d < size)
                 for d, pos, size in ((dt, t, nt), (dx, gx, nx), (dy, gy, ny))]
        parts = [p for p in parts if p is not None]
        return functools.reduce(jnp.logical_and, parts), (t + dt, gx + dx, gy + dy)

    def middle(dx):
        return low != (gx + dx < half)

    def both(*conds):
        conds = [c for c in conds if c is not None]
        return functools.reduce(jnp.logical_and, conds) if conds else None

    peers = []
    for dt in (0, -1, 1):
        for dx, dy in AROUND:
            cond, target = near(dt, dx, dy)
            peers.append((both(cond, jnp.logical_not(middle(dx))) if dt and dx else cond, target))
    peers += [(None, (lax.rem(t + d, nt), gx, gy)) for d in range(1, nt)]
    barrier = pltpu.get_barrier_semaphore()
    expected = jnp.int32(0)
    for cond, target in peers:
        when(cond, functools.partial(pl.semaphore_signal, barrier, inc=1, device_id=target, device_id_type=MESH))
        expected = expected + (1 if cond is None else cond.astype(jnp.int32))

    def clear(cond, *parts):
        def act():
            for ref, index in parts:
                ref[index] = jnp.zeros_like(ref[index])
        pl.when(cond)(act)

    side_rows = slice(None)
    for cond, rows, side in ((gx == 0, slice(0, EDGE), 0), (gx == nx - 1, slice(ROWS, MID), 1)):
        clear(cond, (ff, (side_rows, rows)), (left_in, rows), (right_in, rows), (nxt, rows),
              (fold_in, (slice(None), 2 * side)), (value_near, side))
        pl.when(cond)(functools.partial(
            cell_near.__setitem__, side, jnp.full(cell_near.shape[1:], -1, jnp.int32)))
    clear(gy == 0, (left_in, ...), (fold_in, 0))
    clear(gy == ny - 1, (right_in, ...), (fold_in, 1))
    clear(t == nt - 1, (nxt, ...), (fold_in, ...))

    one = Model(MID, field1, coef1, slope1, path1, adj1, flux1, grad1, gain1, final1)
    two = Model(END, field2, coef2, slope2, path2, adj2, flux2, grad2, gain2, final2)
    again = Model(ROWS, field3, coef1, slope1, path1, adj1, flux1, grad1, gain3, final3)
    rest = Model(END, field2, coef2, slope2, path2, adj2, flux2, grad2, gain2, final4)
    for part in (one, two):
        part.clear_ends()

    loads[0].wait()
    loads[1].wait()
    for j in range(2):
        ff[N0 + j, inner], ff[V0 + j, inner] = counted(cell_in[j, 0], value_in[j, 0], ROWS, 0)
    loads[2].wait()
    loads[3].wait()
    ff[RATE, inner] = jnp.where(mask_in[...] != 0, rate_in[...], 0.0)
    for load in loads[4:]:
        load.wait()

    at = lane((BLOCK, COLS))
    at8 = lane((8, COLS))
    for r in range(0, ROWS, BLOCK):
        to_left = to_right = jnp.zeros((BLOCK, COLS), jnp.float32)
        for f, (start, width) in enumerate(STRIP):
            turned = rolled(ff[f, span(home + r, BLOCK)], start)
            to_left = jnp.where(within(at, start, width), turned, to_left)
            to_right = jnp.where(within(at, start - width, width), turned, to_right)
        left_out[r:r + BLOCK] = to_left
        right_out[r:r + BLOCK] = to_right

    def fold(to, field):
        to_left = to_right = jnp.zeros((8, COLS), jnp.float32)
        for k in range(ROWS // 8):
            turned = rolled(field[span(home + 8 * k, 8)], 16 * k)
            to_left = jnp.where(within(at8, 16 * k, 16), turned, to_left)
            to_right = jnp.where(within(at8, 16 * k - 16, 16), turned, to_right)
        fold_out[to, 0], fold_out[to, 1] = to_left, to_right

    fold(0, ff.at[S0])

    def first_row(dx):
        return ROWS - EDGE if dx > 0 else 0

    copies = []

    def remote(to, target, src, dst):
        i = len(copies)
        copy = pltpu.make_async_remote_copy(
            src_ref=src, dst_ref=dst, send_sem=send_sem.at[i], recv_sem=recv_sem.at[i],
            device_id=target, device_id_type=MESH)
        copies.append((copy, to))
        return copy

    def halo(dt, dx, dy, pick, also_to=None, also_from=None):
        to, target = near(dt, dx, dy)
        come, _ = near(-dt, -dx, -dy)
        to, come = both(to, also_to), both(come, also_from)
        count = EDGE if dx else ROWS
        land = span(place(-dx, gx + dx < half), count)
        return remote(to, target, *pick(span(home + first_row(dx), count), pl.ds(first_row(dx), count), land)), to, come, dx

    def strips(dy):
        out, into = (left_out, right_in) if dy < 0 else (right_out, left_in)
        return lambda own, tile, land: (out.at[tile], into.at[land])

    early = [halo(0, dx, 0, lambda own, tile, land: (ff.at[0:4, own], ff.at[0:4, land])) for dx in (1, -1)]
    early += [halo(0, dx, dy, strips(dy)) for dx, dy in CORNERS + ((0, -1), (0, 1))]
    late = []
    for dx in (1, -1):
        side = 0 if dx > 0 else 1
        late.append(halo(0, dx, 0, lambda own, tile, land: (cell_in, cell_near.at[side])))
        late.append(halo(0, dx, 0, lambda own, tile, land: (value_in, value_near.at[side])))
    def next_slice(i, field, dx, dy):
        if dy == 0:
            return lambda own, tile, land: (field.at[own], nxt.at[land])
        return lambda own, tile, land: (fold_out.at[i, 0 if dy < 0 else 1], fold_in.at[1 if dy < 0 else 0, 1 - dx])

    next_tile = halo(-1, 0, 0, next_slice(0, ff.at[S0], 0, 0))
    for dx, dy in AROUND:
        conds = [None] * 2 if dx == 0 else [jnp.logical_not(middle(d)) for d in (dx, -dx)]
        late.append(halo(-1, dx, dy, next_slice(0, ff.at[S0], dx, dy), *conds))
    for dx in (1, -1):
        late.append(halo(0, dx, 0, lambda own, tile, land: (ff.at[BACK, own], ff.at[BACK, land]), t == 0, t == 0))
    onward = [halo(0, dx, dy, next_slice(1, nxt, dx, dy), *(both(t < nt - 1, middle(d)) for d in (dx, -dx)))
              for dx, dy in AROUND if dx]

    pl.semaphore_wait(barrier, expected)
    for copy, to, _, _ in [next_tile] + early + late:
        when(to, copy.start)
    when(next_tile[2], next_tile[0].wait_recv)

    @pl.when((t < nt - 1) & (middle(1) | middle(-1)))
    def _():
        fold(1, nxt)

    for copy, to, _, _ in onward:
        when(to, copy.start)
    late += onward

    def arrive(group, far):
        for copy, _, come, dx in group:
            if dx:
                when(come & (low if (dx > 0) != far else high), copy.wait_recv)
            elif not far:
                when(come, copy.wait_recv)

    def unpacked(f, rows):
        start, width = STRIP[f]
        return jnp.where(at < width, rolled(right_in[rows], -start),
                         jnp.where(at >= COLS - width, rolled(left_in[rows], -start), 0.0))

    def take(part, r, rows):
        to = slice(r, r + BLOCK)
        for f in range(4):
            part.field[0, f, to] = ff[f, rows]
            part.field[1, f, to] = unpacked(f, rows)

    def unfolded(spots):
        out = []
        for pair in spots:
            which = jnp.where(low, pair[0][0], pair[1][0])
            left, right = fold_in[0, which], fold_in[1, which]
            got = [jnp.where(at8 < 16, rolled(right, -16 * k), jnp.where(at8 >= COLS - 16, rolled(left, -16 * k), 0.0))
                   for _, k in pair]
            out.append(jnp.where(low, *got))
        return jnp.concatenate(out, axis=0)

    more = (t < nt - 1).astype(jnp.float32)

    def demand(part, pulls, back, foll, r, rows, spots):
        to = slice(r, r + BLOCK)
        back[0, to], back[1, to] = ff[BACK, rows], unpacked(BACK, rows)
        for p in range(2):
            got = [ff[f, rows] if p == 0 else unpacked(f, rows) for f in (N0, N1, V0, V1)]
            following = nxt[rows] if p == 0 else unfolded(spots)
            foll[p, to] = following
            part.gain[p, 0, to], part.gain[p, 1, to] = got[0] + 1.0, got[1] + more
            pulls[p, 0, to], pulls[p, 1, to] = got[2], got[3]
            part.adj[p, 0, to] = got[2] + part.field[p, S1, to]
            part.adj[p, 1, to] = got[3] + following

    def beside(far):
        from_up = low if not far else high
        side, skip = jnp.where(from_up, 0, 1), jnp.where(from_up, ROWS - EDGE, 0)
        rows = span(MID if far else jnp.where(low, 0, ROWS), EDGE)
        for j in range(2):
            ff[N0 + j, rows], ff[V0 + j, rows] = counted(cell_near[side, j, 0], value_near[side, j, 0], EDGE, skip)

    arrive(early, False)
    for r in range(0, MID, BLOCK):
        take(one, r, slice(r, r + BLOCK))
    one.coefficients()
    one.slopes()
    for k in range(STEPS):
        one.forward(k)
    before, after = near(-1, 0, 0), near(1, 0, 0)

    def pack(to, groups, get):
        packed = jnp.zeros((8, COLS), jnp.float32)
        for k in range(groups):
            main, side = get(8 + 8 * k)
            to[8 * k:8 * k + 8] = main
            packed = jnp.where(within(at8, 16 * k - 8, 16), rolled(side, 16 * k), packed)
        to[8 * groups:8 * groups + 8] = packed

    def unpack(ref, groups, k):
        side = rolled(ref[8 * groups:8 * groups + 8], -16 * k)
        return ref[8 * k:8 * k + 8], jnp.where(within(at8, -8, 16), side, 0.0)

    def send_final(part, to, into):
        pack(to, (part.rows - 16) // 8, lambda r: [part.final[p, 1, r:r + 8] for p in range(2)])
        copy = remote(*after, to, into)
        when(after[0], copy.start)
        return copy

    def send_adjoint(part, to, into):
        pack(to, (part.rows - 16) // 8, lambda r: [part.adj[p, 0, r:r + 8] for p in range(2)])
        copy = remote(*before, to, into)
        when(before[0], copy.start)
        return copy

    fin_copies = [send_final(one, fin_out1, fin1)]
    arrive(late, False)
    beside(False)
    for r in range(0, MID, BLOCK):
        spots = []
        for g in (r // 8, r // 8 + 1):
            spots.append([(0, 6 + g) if g < 2 else (1, g - 2), (1, g) if g < 8 else (2, g - 8)])
        demand(one, pull1, back1, foll1, r, slice(r, r + BLOCK), spots)
    one.force()

    dest1, dest2 = jnp.where(low, 0, EDGE), jnp.where(low, ROWS, 0)
    one.pull()

    def broadcast(buffer):
        out = []
        for d in sorted(range(1, nt), key=lambda d: -min(d, nt - d)):
            out.append(remote(None, (lax.rem(t + d, nt), gx, gy), buffer.at[t], buffer.at[t]))
        for copy in out:
            copy.start()
        return out

    def put_bed_gradient(part, buffer):
        pack(buffer.at[t], (part.rows - 16) // 8, lambda r: part.bed_gradient(r, 8))
        return broadcast(buffer)

    odd = lax.rem(t, 2)
    pack(mine, ROWS // 8, lambda r: one.bed_gradient(r, 8))
    to_partner = remote(None, (t + 1 - 2 * odd, gx, gy), mine, theirs)
    to_partner.start()

    spots2 = [[[(1, 6), (0, 6)], [(1, 7), (0, 7)]], [[(2, 0), (1, 0)], [(2, 1), (1, 1)]]]
    from2 = [span(jnp.where(low, ROWS, MID), BLOCK), span(jnp.where(low, MID, 0), BLOCK)]
    arrive(early, True)
    for i in range(2):
        take(two, BLOCK * i, from2[i])
    two.coefficients()
    two.slopes()
    for k in range(STEPS):
        two.forward(k)
    fin_copies.append(send_final(two, fin_out2, fin2))
    arrive(late, True)
    beside(True)
    for i in range(2):
        demand(two, pull2, back2, foll2, BLOCK * i, from2[i], spots2[i])
    two.force()
    two.pull()
    sent2 = put_bed_gradient(two, sums2)
    to_partner.wait_recv()
    pair = t // 2
    pairs[pair] = mine[...] + theirs[...]
    exchanged = []
    for far in range(nt // 2 - 1, 0, -1):
        for parity in range(2):
            off = min((2 * far - parity) % nt, (2 * far + 1 - parity) % nt, key=lambda o: min(o, nt - o))
            copy = remote(odd == (parity + off) % 2, (lax.rem(t + nt - off, nt), gx, gy), pairs.at[pair], pairs.at[pair])
            exchanged.append((copy, odd == parity))
            when(odd == (parity + off) % 2, copy.start)
    lam_copies = [send_adjoint(one, lam_out1, lam1), send_adjoint(two, lam_out2, lam2)]

    for copy in fin_copies:
        when(before[0], copy.wait_recv)
    parts = ((one, pull1, back1, foll1, fin1, lam1, dest1), (two, pull2, back2, foll2, fin2, lam2, dest2))
    for part, pulls, back, foll, fin, lam, dest in parts:
        groups = (part.rows - 16) // 8
        for k in range(groups):
            rows, to = slice(8 + 8 * k, 16 + 8 * k), span(dest + 8 * k, 8)
            for p, came in enumerate(unpack(fin, groups, k)):
                begun = jnp.where(t == 0, back[p, rows], came)
                s0, s1 = part.field[p, S0, rows], part.field[p, S1, rows]
                field3[p, S0, to] = s0 - STATE_RATE * ((s0 - begun) + part.adj[p, 0, rows])
                field3[p, S1, to] = s1 - STATE_RATE * ((s1 - part.final[p, 0, rows]) + part.adj[p, 1, rows])
                field3[p, RATE, to] = part.field[p, RATE, rows]
                gain3[p, :, to] = part.gain[p, :, rows]
    again.coefficients()

    def to_rest(*fields):
        for p in range(2):
            for f in fields:
                field2[p, f, 0:END] = field3[p, f, MID - END:MID]

    to_rest(S0, S1, RATE)
    gain2[...] = gain3[:, :, MID - END:MID]
    rest.coefficients()

    def total(ref, rows):
        got = ref[0, rows]
        for i in range(1, ref.shape[0]):
            got = got + ref[i, rows]
        return got

    for copy, come in exchanged:
        when(come, copy.wait_recv)
    for copy in sent2:
        copy.wait_recv()
    for part, sums, dest in ((one, pairs, dest1), (two, sums2, dest2)):
        groups = (part.rows - 16) // 8
        sides = total(sums, slice(8 * groups, 8 * groups + 8))
        for k in range(groups):
            rows, to = slice(8 + 8 * k, 16 + 8 * k), span(dest + 8 * k, 8)
            main = total(sums, slice(8 * k, 8 * k + 8))
            side = jnp.where(within(at8, -8, 16), rolled(sides, -16 * k), 0.0)
            for p, got in enumerate((main, side)):
                field3[p, BED, to] = part.field[p, BED, rows] - BED_RATE * got
    to_rest(BED)

    again.slopes()
    for k in range(STEPS):
        again.forward(k)
    split = ROWS - EDGE
    fin_copies = [remote(*after, final3.at[0, 1, 8:8 + split], fin_last.at[0:split])]
    when(after[0], fin_copies[0].start)
    for copy in lam_copies:
        when(after[0], copy.wait_recv)
    for part, pulls, back, foll, fin, lam, dest in parts:
        groups = (part.rows - 16) // 8
        for k in range(groups):
            rows, to = slice(8 + 8 * k, 16 + 8 * k), span(dest + 8 * k, 8)
            for p, came in enumerate(unpack(lam, groups, k)):
                old = foll[p, rows]
                new = old - STATE_RATE * ((old - part.final[p, 1, rows]) + came)
                pull3[p, 0, to] = pulls[p, 0, rows] + field3[p, S1, to]
                pull3[p, 1, to] = pulls[p, 1, rows] + jnp.where(t < nt - 1, new, 0.0)

    for p in range(2):
        adj1[p, :, 0:ROWS] = pull3[p, :, 0:ROWS]
    again.force()
    again.pull()
    for r in range(0, split, BLOCK):
        sums3[t, r:r + BLOCK] = again.bed_gradient(8 + r, BLOCK)[0]
    sent3 = broadcast(sums3)

    for p in range(2):
        adj2[p, :, 0:END] = pull3[p, :, MID - END:MID]
    rest.slopes()
    for k in range(STEPS):
        rest.forward(k)
    fin_copies.append(remote(*after, final4.at[0, 1, 8:8 + EDGE], fin_last.at[split:ROWS]))
    when(after[0], fin_copies[1].start)
    rest.force()
    rest.pull()
    sums4[t] = rest.bed_gradient(8, EDGE)[0]
    sent4 = broadcast(sums4)

    for copy in fin_copies:
        when(before[0], copy.wait_recv)
    for r in range(0, ROWS, BLOCK):
        rows, short = slice(8 + r, 8 + r + BLOCK), slice(r, r + BLOCK)
        part, own = (again, rows) if r < split else (rest, slice(8, 8 + EDGE))
        begun = jnp.where(t == 0, ff[BACK, span(home + r, BLOCK)], fin_last[short])
        s0, s1 = field3[0, S0, rows], field3[0, S1, rows]
        states_out[0, short] = s0 - STATE_RATE * ((s0 - begun) + part.adj[0, 0, own])
        states_out[1, short] = s1 - STATE_RATE * ((s1 - part.final[0, 0, own]) + part.adj[0, 1, own])
    for copy in sent3 + sent4:
        copy.wait_recv()
    for r in range(0, ROWS, BLOCK):
        rows, short = slice(8 + r, 8 + r + BLOCK), slice(r, r + BLOCK)
        now = field3[0, BED, rows]
        sums = total(sums3, short) if r < split else total(sums4, slice(0, EDGE))
        bed_out[short] = now - BED_RATE * (sums + (now - ff[BED, span(home + r, BLOCK)]))
    for copy, to in copies:
        when(to, copy.wait_send)


def emit(states, bed, states_out, bed_out, sem):
    copies = [pltpu.make_async_copy(src, dst, sem.at[i]) for i, (src, dst) in enumerate(((states, states_out), (bed, bed_out)))]
    for copy in copies:
        copy.start()
    for copy in copies:
        copy.wait()


def solution(mesh):
    nt, nx, ny = (mesh.shape[a] for a in ("tm", "gx", "gy"))
    f32 = jnp.float32

    def vmem(*shape, dtype=f32):
        return pltpu.VMEM(shape, dtype)

    def model_scratch(rows):
        return [
            vmem(2, 4, rows + 8, COLS), vmem(2, 2, rows, COLS), vmem(2, 2, rows, COLS),
            vmem(STEPS - 1, 2, 2, rows + 8, COLS), vmem(2, 2, rows + 8, COLS), vmem(2, 2, 8 + rows, COLS),
            vmem(2, 2, 8 + rows, COLS), vmem(2, 2, rows, COLS), vmem(2, 2, rows, COLS),
        ]

    def step(states, bed, background, mask, rate, cells, values):
        obs = cells.shape[-1]
        count = 23 + 6 + 2 + 2 + 2 + 1 + 2 * (nt // 2 - 1) + 3 * (nt - 1)
        out = pl.pallas_call(
            functools.partial(kernel, nt, nx, ny),
            out_shape=(pltpu.VMEM(states.shape, f32), pltpu.VMEM(bed.shape, f32)),
            out_specs=(pl.BlockSpec(memory_space=pltpu.VMEM),) * 2,
            in_specs=[pl.BlockSpec(memory_space=pltpu.HBM)] * 7,
            scratch_shapes=[
                vmem(FIELDS, HIGH, COLS),
                vmem(ROWS, COLS), vmem(ROWS, COLS, dtype=jnp.int32),
                vmem(2, 1, 1, obs, dtype=jnp.int32), vmem(2, 1, 1, obs),
                vmem(2, 2, 1, 1, obs, dtype=jnp.int32), vmem(2, 2, 1, 1, obs),
                vmem(ROWS, COLS), vmem(ROWS, COLS), vmem(HIGH, COLS), vmem(HIGH, COLS),
                vmem(HIGH, COLS), vmem(2, 2, 8, COLS), vmem(2, 3, 8, COLS), vmem(2, MID, COLS), vmem(2, END, COLS),
                *model_scratch(MID), *model_scratch(END),
                vmem(2, 4, MID + 8, COLS), vmem(2, 2, MID, COLS), vmem(2, 2, ROWS, COLS), vmem(2, 2, END, COLS),
                vmem(2, 2, MID, COLS), vmem(2, 2, END, COLS), vmem(2, 2, MID, COLS),
                vmem(2, MID, COLS), vmem(2, END, COLS),
                vmem(ROWS + 8, COLS), vmem(ROWS + 8, COLS), vmem(nt // 2, ROWS + 8, COLS), vmem(nt, EDGE + 8, COLS),
                vmem(nt, ROWS - EDGE, COLS), vmem(nt, EDGE, COLS),
                vmem(ROWS + 8, COLS), vmem(EDGE + 8, COLS), vmem(ROWS + 8, COLS), vmem(EDGE + 8, COLS), vmem(ROWS, COLS),
                vmem(ROWS + 8, COLS), vmem(EDGE + 8, COLS), vmem(ROWS + 8, COLS), vmem(EDGE + 8, COLS),
                pltpu.SemaphoreType.DMA((7,)),
                pltpu.SemaphoreType.DMA((count,)), pltpu.SemaphoreType.DMA((count,)),
            ],
            compiler_params=pltpu.CompilerParams(
                collective_id=0, has_side_effects=True, vmem_limit_bytes=32 << 20),
            name="assimilate",
        )(*(pltpu.with_memory_space_constraint(x, pltpu.HBM)
            for x in (states, bed, background, mask, rate, cells, values)))
        return pl.pallas_call(
            emit,
            out_shape=(jax.ShapeDtypeStruct(states.shape, f32), jax.ShapeDtypeStruct(bed.shape, f32)),
            in_specs=[pl.BlockSpec(memory_space=pltpu.VMEM)] * 2,
            out_specs=(pl.BlockSpec(memory_space=pl.ANY),) * 2,
            scratch_shapes=[pltpu.SemaphoreType.DMA((2,))],
            compiler_params=pltpu.CompilerParams(vmem_limit_bytes=1 << 20),
            name="emit",
        )(*(pltpu.with_memory_space_constraint(x, pltpu.VMEM) for x in out))

    return jax.shard_map(
        step,
        mesh=mesh,
        in_specs=(P("tm", "gx", "gy"),) + (P("gx", "gy"),) * 4 + (P("tm", "gx", "gy", None),) * 2,
        out_specs=(P("tm", "gx", "gy"), P("gx", "gy")),
        check_vma=False,
    )
```

```python
import functools

import jax
import jax.numpy as jnp
from jax import lax
from jax.experimental import pallas as pl
from jax.experimental.pallas import tpu as pltpu
from jax.sharding import PartitionSpec as P

STEPS = 4
ROWS, COLS = 64, 128
EDGE = 16
HIGH = ROWS + 2 * EDGE
MID = ROWS + EDGE
END = 2 * EDGE
BLOCK = 16
BED_RATE = 0.1
STATE_RATE = 0.5
MESH = pl.DeviceIdType.MESH

BED, S0, S1, RATE, N0, N1, V0, V1, BACK = range(9)
FIELDS = 9
STRIP = ((0, 16), (16, 16), (32, 16), (48, 16), (64, 12), (76, 12), (88, 12), (100, 12), (112, 8))
CORNERS = ((1, -1), (1, 1), (-1, -1), (-1, 1))
AROUND = ((1, 0), (-1, 0)) + CORNERS + ((0, -1), (0, 1))


def when(cond, act):
    if cond is None:
        act()
    else:
        pl.when(cond)(act)


def span(start, size):
    return pl.ds(pl.multiple_of(start, 8), size)


def rolled(value, shift):
    shift %= COLS
    return value if shift == 0 else pltpu.roll(value, shift, value.ndim - 1)


def lane(shape):
    return lax.broadcasted_iota(jnp.int32, shape, len(shape) - 1)


def ahead(main, side):
    last = lane(main.shape) == COLS - 1
    main, side = rolled(main, -1), rolled(side, -1)
    return jnp.where(last, side, main), jnp.where(last, main, side)


def behind(main, side):
    first = lane(main.shape) == 0
    main, side = rolled(main, 1), rolled(side, 1)
    return jnp.where(first, side, main), jnp.where(first, main, side)


def within(at, start, width):
    start %= COLS
    if start + width <= COLS:
        return (at >= start) & (at < start + width)
    return (at >= start) | (at < start + width - COLS)


def counted(cell, value, rows, skip):
    obs = cell.shape[-1]
    row, col = cell // COLS - skip, cell % COLS
    in_row = (lax.broadcasted_iota(jnp.int32, (rows, obs), 0) == row).astype(jnp.float32)
    in_col = (lax.broadcasted_iota(jnp.int32, (COLS, obs), 0) == col).astype(jnp.float32).astype(jnp.bfloat16)
    parts = [in_row.astype(jnp.bfloat16)]
    rest = value
    for _ in range(3):
        part = rest.astype(jnp.bfloat16)
        rest = rest - part.astype(jnp.float32)
        parts.append((in_row * part.astype(jnp.float32)).astype(jnp.bfloat16))
    got = lax.dot_general(jnp.concatenate(parts, axis=0), in_col, (((1,), (1,)), ((), ())),
                          preferred_element_type=jnp.float32)
    return got[:rows], (got[3 * rows:] + got[2 * rows:3 * rows]) + got[rows:2 * rows]


class Model:
    def __init__(self, rows, field, coef, slope, path, adj, flux, grad, gain, final):
        self.rows, self.field, self.coef, self.slope, self.path = rows, field, coef, slope, path
        self.adj, self.flux, self.grad, self.gain, self.final = adj, flux, grad, gain, final

    def blocks(self):
        return [slice(r, r + BLOCK) for r in range(0, self.rows, BLOCK)]

    def clear_ends(self):
        tail = slice(self.rows, self.rows + 8)
        for ref, index in ((self.field, (Ellipsis, tail, slice(None))), (self.path, (Ellipsis, tail, slice(None))),
                           (self.adj, (Ellipsis, tail, slice(None))), (self.flux, (Ellipsis, slice(0, 8), slice(None))),
                           (self.grad, (Ellipsis, slice(0, 8), slice(None)))):
            ref[index] = jnp.zeros_like(ref[index])

    def coefficients(self):
        def mean_rate(a, b):
            return jnp.where(jnp.minimum(a, b) > 0.0, 0.5 * (a + b), 0.0)

        for rows in self.blocks():
            both = [self.field[p, RATE, rows] for p in range(2)]
            for p, (here, up) in enumerate(zip(both, ahead(*both))):
                self.coef[1, p, rows] = mean_rate(here, up)
                self.coef[0, p, rows] = mean_rate(here, self.field[p, RATE, rows.start + 1:rows.stop + 1])

    def slopes(self):
        for rows in self.blocks():
            both = [self.field[p, BED, rows] for p in range(2)]
            for p, (here, up) in enumerate(zip(both, ahead(*both))):
                self.slope[1, p, rows] = up - here
                self.slope[0, p, rows] = self.field[p, BED, rows.start + 1:rows.stop + 1] - here

    def thick(self, k, p, rows):
        return self.field[p, S0:S1 + 1, rows] if k == 0 else self.path[k - 1, p, :, rows]

    def faces(self, k, rows):
        here = [self.thick(k, p, rows) for p in range(2)]
        up = [[self.thick(k, p, slice(rows.start + 1, rows.stop + 1)) for p in range(2)], ahead(*here)]
        mean = [[0.5 * (here[p] + up[d][p]) for p in range(2)] for d in range(2)]
        step = [[(up[d][p] - here[p]) + self.slope[d, p, rows] for p in range(2)] for d in range(2)]
        return here, mean, step

    def forward(self, k):
        for rows in self.blocks():
            here, mean, step = self.faces(k, rows)
            f = [[self.coef[d, p, rows] * mean[d][p] * mean[d][p] * step[d][p] for p in range(2)] for d in range(2)]
            left = behind(*f[1])
            for p in range(2):
                self.flux[p, :, 8 + rows.start:8 + rows.stop] = f[0][p]
                new = here[p] + ((f[0][p] - self.flux[p, :, 7 + rows.start:7 + rows.stop]) + (f[1][p] - left[p]))
                if k + 1 < STEPS:
                    self.path[k, p, :, rows] = new
                else:
                    self.final[p, :, rows] = new

    def force(self):
        for rows in self.blocks():
            for p in range(2):
                self.adj[p, :, rows] = self.gain[p, :, rows] * self.final[p, :, rows] - self.adj[p, :, rows]

    def backward(self, k):
        for rows in self.blocks():
            _, mean, step = self.faces(k, rows)
            lam = [self.adj[p, :, rows] for p in range(2)]
            up = [[self.adj[p, :, rows.start + 1:rows.stop + 1] for p in range(2)], ahead(*lam)]
            spot = slice(8 + rows.start, 8 + rows.stop)
            keep, give = [[], []], [[], []]
            for d in range(2):
                for p in range(2):
                    q = self.coef[d, p, rows] * mean[d][p] * (lam[p] - up[d][p])
                    g, e = q * mean[d][p], q * step[d][p]
                    keep[d].append(e - g)
                    give[d].append(e + g)
                    both = g[0] + g[1]
                    self.grad[d, p, spot] = both if k == STEPS - 1 else self.grad[d, p, spot] + both
            given = behind(*give[1])
            for p in range(2):
                self.flux[p, :, spot] = give[0][p]
                self.adj[p, :, rows] = (
                    lam[p] + (keep[0][p] + self.flux[p, :, 7 + rows.start:7 + rows.stop]) + (keep[1][p] + given[p]))

    def pull(self):
        for k in reversed(range(STEPS)):
            self.backward(k)

    def bed_gradient(self, r, count):
        spot, before = slice(8 + r, 8 + r + count), slice(7 + r, 7 + r + count)
        left = behind(self.grad[1, 0, spot], self.grad[1, 1, spot])
        return [(self.grad[0, p, before] - self.grad[0, p, spot]) + (left[p] - self.grad[1, p, spot]) for p in range(2)]


def kernel(
    nt, nx, ny,
    states, bed, background, mask, rate, cells, values,
    states_out, bed_out,
    ff, rate_in, mask_in, cell_in, value_in, cell_near, value_near, left_out, right_out, left_in, right_in,
    nxt, fold_out, fold_in, foll1, foll2,
    field1, coef1, slope1, path1, adj1, flux1, grad1, gain1, final1,
    field2, coef2, slope2, path2, adj2, flux2, grad2, gain2, final2,
    field3, gain3, final3, field4, gain4, final4,
    pull1, pull2, pull3, pull4, back1, back2,
    mine, theirs, pairs, sums2, sums3, sums4, fin_out1, fin_out2, fin1, fin2, fin3, fin4, lam_out1, lam_out2, lam1, lam2,
    load_sem, send_sem, recv_sem,
):
    t, gx, gy = lax.axis_index("tm"), lax.axis_index("gx"), lax.axis_index("gy")
    half = nx // 2
    low = gx < half
    high = jnp.logical_not(low)

    def place(side, is_low):
        return jnp.where(is_low, *{-1: (0, MID), 0: (EDGE, 0), 1: (MID, ROWS)}[side])

    home = place(0, low)
    inner = span(home, ROWS)

    loads = [
        pltpu.make_async_copy(src, dst, load_sem.at[i])
        for i, (src, dst) in enumerate((
            (cells, cell_in), (values, value_in), (mask, mask_in), (rate, rate_in),
            (states, ff.at[S0:S1 + 1, inner]), (bed, ff.at[BED, inner]), (background, ff.at[BACK, inner]),
        ))
    ]
    for load in loads:
        load.start()

    def near(dt, dx, dy):
        parts = [None if d == 0 else (pos + d >= 0) & (pos + d < size)
                 for d, pos, size in ((dt, t, nt), (dx, gx, nx), (dy, gy, ny))]
        parts = [p for p in parts if p is not None]
        return functools.reduce(jnp.logical_and, parts), (t + dt, gx + dx, gy + dy)

    def middle(dx):
        return low != (gx + dx < half)

    def both(*conds):
        conds = [c for c in conds if c is not None]
        return functools.reduce(jnp.logical_and, conds) if conds else None

    peers = []
    for dt in (0, -1, 1):
        for dx, dy in AROUND:
            cond, target = near(dt, dx, dy)
            peers.append((both(cond, jnp.logical_not(middle(dx))) if dt and dx else cond, target))
    peers += [(None, (lax.rem(t + d, nt), gx, gy)) for d in range(1, nt)]
    barrier = pltpu.get_barrier_semaphore()
    expected = jnp.int32(0)
    for cond, target in peers:
        when(cond, functools.partial(pl.semaphore_signal, barrier, inc=1, device_id=target, device_id_type=MESH))
        expected = expected + (1 if cond is None else cond.astype(jnp.int32))

    def clear(cond, *parts):
        def act():
            for ref, index in parts:
                ref[index] = jnp.zeros_like(ref[index])
        pl.when(cond)(act)

    side_rows = slice(None)
    for cond, rows, side in ((gx == 0, slice(0, EDGE), 0), (gx == nx - 1, slice(ROWS, MID), 1)):
        clear(cond, (ff, (side_rows, rows)), (left_in, rows), (right_in, rows), (nxt, rows),
              (fold_in, (slice(None), 2 * side)), (value_near, side))
        pl.when(cond)(functools.partial(
            cell_near.__setitem__, side, jnp.full(cell_near.shape[1:], -1, jnp.int32)))
    clear(gy == 0, (left_in, ...), (fold_in, 0))
    clear(gy == ny - 1, (right_in, ...), (fold_in, 1))
    clear(t == nt - 1, (nxt, ...), (fold_in, ...))

    one = Model(MID, field1, coef1, slope1, path1, adj1, flux1, grad1, gain1, final1)
    two = Model(END, field2, coef2, slope2, path2, adj2, flux2, grad2, gain2, final2)
    again = Model(ROWS, field3, coef1, slope1, path1, adj1, flux1, grad1, gain3, final3)
    rest = Model(END, field4, coef2, slope2, path2, adj2, flux2, grad2, gain4, final4)
    for part in (one, two, again, rest):
        part.clear_ends()

    loads[0].wait()
    loads[1].wait()
    for j in range(2):
        ff[N0 + j, inner], ff[V0 + j, inner] = counted(cell_in[j, 0], value_in[j, 0], ROWS, 0)
    loads[2].wait()
    loads[3].wait()
    ff[RATE, inner] = jnp.where(mask_in[...] != 0, rate_in[...], 0.0)
    for load in loads[4:]:
        load.wait()

    at = lane((BLOCK, COLS))
    at8 = lane((8, COLS))
    for r in range(0, ROWS, BLOCK):
        to_left = to_right = jnp.zeros((BLOCK, COLS), jnp.float32)
        for f, (start, width) in enumerate(STRIP):
            turned = rolled(ff[f, span(home + r, BLOCK)], start)
            to_left = jnp.where(within(at, start, width), turned, to_left)
            to_right = jnp.where(within(at, start - width, width), turned, to_right)
        left_out[r:r + BLOCK] = to_left
        right_out[r:r + BLOCK] = to_right

    def fold(to, field):
        to_left = to_right = jnp.zeros((8, COLS), jnp.float32)
        for k in range(ROWS // 8):
            turned = rolled(field[span(home + 8 * k, 8)], 16 * k)
            to_left = jnp.where(within(at8, 16 * k, 16), turned, to_left)
            to_right = jnp.where(within(at8, 16 * k - 16, 16), turned, to_right)
        fold_out[to, 0], fold_out[to, 1] = to_left, to_right

    fold(0, ff.at[S0])

    def first_row(dx):
        return ROWS - EDGE if dx > 0 else 0

    copies = []

    def remote(to, target, src, dst):
        i = len(copies)
        copy = pltpu.make_async_remote_copy(
            src_ref=src, dst_ref=dst, send_sem=send_sem.at[i], recv_sem=recv_sem.at[i],
            device_id=target, device_id_type=MESH)
        copies.append((copy, to))
        return copy

    def halo(dt, dx, dy, pick, also_to=None, also_from=None):
        to, target = near(dt, dx, dy)
        come, _ = near(-dt, -dx, -dy)
        to, come = both(to, also_to), both(come, also_from)
        count = EDGE if dx else ROWS
        land = span(place(-dx, gx + dx < half), count)
        return remote(to, target, *pick(span(home + first_row(dx), count), pl.ds(first_row(dx), count), land)), to, come, dx

    def strips(dy):
        out, into = (left_out, right_in) if dy < 0 else (right_out, left_in)
        return lambda own, tile, land: (out.at[tile], into.at[land])

    early = [halo(0, dx, 0, lambda own, tile, land: (ff.at[0:4, own], ff.at[0:4, land])) for dx in (1, -1)]
    early += [halo(0, dx, dy, strips(dy)) for dx, dy in CORNERS + ((0, -1), (0, 1))]
    late = []
    for dx in (1, -1):
        side = 0 if dx > 0 else 1
        late.append(halo(0, dx, 0, lambda own, tile, land: (cell_in, cell_near.at[side])))
        late.append(halo(0, dx, 0, lambda own, tile, land: (value_in, value_near.at[side])))
    def next_slice(i, field, dx, dy):
        if dy == 0:
            return lambda own, tile, land: (field.at[own], nxt.at[land])
        return lambda own, tile, land: (fold_out.at[i, 0 if dy < 0 else 1], fold_in.at[1 if dy < 0 else 0, 1 - dx])

    next_tile = halo(-1, 0, 0, next_slice(0, ff.at[S0], 0, 0))
    for dx, dy in AROUND:
        conds = [None] * 2 if dx == 0 else [jnp.logical_not(middle(d)) for d in (dx, -dx)]
        late.append(halo(-1, dx, dy, next_slice(0, ff.at[S0], dx, dy), *conds))
    for dx in (1, -1):
        late.append(halo(0, dx, 0, lambda own, tile, land: (ff.at[BACK, own], ff.at[BACK, land]), t == 0, t == 0))
    onward = [halo(0, dx, dy, next_slice(1, nxt, dx, dy), *(both(t < nt - 1, middle(d)) for d in (dx, -dx)))
              for dx, dy in AROUND if dx]

    pl.semaphore_wait(barrier, expected)
    for copy, to, _, _ in [next_tile] + early + late:
        when(to, copy.start)
    when(next_tile[2], next_tile[0].wait_recv)

    @pl.when((t < nt - 1) & (middle(1) | middle(-1)))
    def _():
        fold(1, nxt)

    for copy, to, _, _ in onward:
        when(to, copy.start)

    def arrive(group, far):
        for copy, _, come, dx in group:
            if dx:
                when(come & (low if (dx > 0) != far else high), copy.wait_recv)
            elif not far:
                when(come, copy.wait_recv)

    def unpacked(f, rows):
        start, width = STRIP[f]
        return jnp.where(at < width, rolled(right_in[rows], -start),
                         jnp.where(at >= COLS - width, rolled(left_in[rows], -start), 0.0))

    def take(part, r, rows):
        to = slice(r, r + BLOCK)
        for f in range(4):
            part.field[0, f, to] = ff[f, rows]
            part.field[1, f, to] = unpacked(f, rows)

    def unfolded(spots):
        out = []
        for pair in spots:
            which = jnp.where(low, pair[0][0], pair[1][0])
            left, right = fold_in[0, which], fold_in[1, which]
            got = [jnp.where(at8 < 16, rolled(right, -16 * k), jnp.where(at8 >= COLS - 16, rolled(left, -16 * k), 0.0))
                   for _, k in pair]
            out.append(jnp.where(low, *got))
        return jnp.concatenate(out, axis=0)

    more = (t < nt - 1).astype(jnp.float32)

    def demand(part, pulls, back, foll, r, rows, spots):
        to = slice(r, r + BLOCK)
        back[0, to], back[1, to] = ff[BACK, rows], unpacked(BACK, rows)
        for p in range(2):
            got = [ff[f, rows] if p == 0 else unpacked(f, rows) for f in (N0, N1, V0, V1)]
            following = nxt[rows] if p == 0 else unfolded(spots)
            foll[p, to] = following
            part.gain[p, 0, to], part.gain[p, 1, to] = got[0] + 1.0, got[1] + more
            pulls[p, 0, to], pulls[p, 1, to] = got[2], got[3]
            part.adj[p, 0, to] = got[2] + part.field[p, S1, to]
            part.adj[p, 1, to] = got[3] + following

    def beside(far):
        from_up = low if not far else high
        side, skip = jnp.where(from_up, 0, 1), jnp.where(from_up, ROWS - EDGE, 0)
        rows = span(MID if far else jnp.where(low, 0, ROWS), EDGE)
        for j in range(2):
            ff[N0 + j, rows], ff[V0 + j, rows] = counted(cell_near[side, j, 0], value_near[side, j, 0], EDGE, skip)

    arrive(early, False)
    for r in range(0, MID, BLOCK):
        take(one, r, slice(r, r + BLOCK))
    one.coefficients()
    one.slopes()
    for k in range(STEPS):
        one.forward(k)
    before, after = near(-1, 0, 0), near(1, 0, 0)

    def pack(to, groups, get):
        packed = jnp.zeros((8, COLS), jnp.float32)
        for k in range(groups):
            main, side = get(8 + 8 * k)
            to[8 * k:8 * k + 8] = main
            packed = jnp.where(within(at8, 16 * k - 8, 16), rolled(side, 16 * k), packed)
        to[8 * groups:8 * groups + 8] = packed

    def unpack(ref, groups, k):
        side = rolled(ref[8 * groups:8 * groups + 8], -16 * k)
        return ref[8 * k:8 * k + 8], jnp.where(within(at8, -8, 16), side, 0.0)

    def send_final(part, to, into):
        pack(to, (part.rows - 16) // 8, lambda r: [part.final[p, 1, r:r + 8] for p in range(2)])
        copy = remote(*after, to, into)
        when(after[0], copy.start)
        return copy

    def send_adjoint(part, to, into):
        pack(to, (part.rows - 16) // 8, lambda r: [part.adj[p, 0, r:r + 8] for p in range(2)])
        copy = remote(*before, to, into)
        when(before[0], copy.start)
        return copy

    fin_copies = [send_final(one, fin_out1, fin1)]
    arrive(late, False)
    beside(False)
    for r in range(0, MID, BLOCK):
        spots = []
        for g in (r // 8, r // 8 + 1):
            spots.append([(0, 6 + g) if g < 2 else (1, g - 2), (1, g) if g < 8 else (2, g - 8)])
        demand(one, pull1, back1, foll1, r, slice(r, r + BLOCK), spots)
    one.force()

    one.pull()

    def broadcast(buffer):
        out = []
        for d in sorted(range(1, nt), key=lambda d: -min(d, nt - d)):
            out.append(remote(None, (lax.rem(t + d, nt), gx, gy), buffer.at[t], buffer.at[t]))
        for copy in out:
            copy.start()
        return out

    def put_bed_gradient(part, buffer):
        pack(buffer.at[t], (part.rows - 16) // 8, lambda r: part.bed_gradient(r, 8))
        return broadcast(buffer)

    odd = lax.rem(t, 2)
    pack(mine, ROWS // 8, lambda r: one.bed_gradient(r, 8))
    to_partner = remote(None, (t + 1 - 2 * odd, gx, gy), mine, theirs)
    to_partner.start()

    spots2 = [[[(1, 6), (0, 6)], [(1, 7), (0, 7)]], [[(2, 0), (1, 0)], [(2, 1), (1, 1)]]]
    from2 = [span(jnp.where(low, ROWS, MID), BLOCK), span(jnp.where(low, MID, 0), BLOCK)]
    arrive(early, True)
    for i in range(2):
        take(two, BLOCK * i, from2[i])
    two.coefficients()
    two.slopes()
    for k in range(STEPS):
        two.forward(k)
    fin_copies.append(send_final(two, fin_out2, fin2))
    arrive(late, True)
    beside(True)
    arrive(onward, True)
    for i in range(2):
        demand(two, pull2, back2, foll2, BLOCK * i, from2[i], spots2[i])
    two.force()
    two.pull()
    sent2 = put_bed_gradient(two, sums2)
    to_partner.wait_recv()
    pair = t // 2
    pairs[pair] = mine[...] + theirs[...]
    exchanged = []
    for far in range(nt // 2 - 1, 0, -1):
        for parity in range(2):
            off = min((2 * far - parity) % nt, (2 * far + 1 - parity) % nt, key=lambda o: min(o, nt - o))
            copy = remote(odd == (parity + off) % 2, (lax.rem(t + nt - off, nt), gx, gy), pairs.at[pair], pairs.at[pair])
            exchanged.append((copy, odd == parity))
            when(odd == (parity + off) % 2, copy.start)
    lam_copies = [send_adjoint(one, lam_out1, lam1), send_adjoint(two, lam_out2, lam2)]

    def renew(part, pulls, back, foll, fin, lam, field, gain, pull, start):
        groups = (part.rows - 16) // 8
        for k in range(groups):
            rows, to = slice(8 + 8 * k, 16 + 8 * k), span(start + 8 * k, 8)
            came, came_lam = unpack(fin, groups, k), unpack(lam, groups, k)
            for p in range(2):
                begun = jnp.where(t == 0, back[p, rows], came[p])
                s0, s1 = part.field[p, S0, rows], part.field[p, S1, rows]
                field[p, S0, to] = s0 - STATE_RATE * ((s0 - begun) + part.adj[p, 0, rows])
                new1 = s1 - STATE_RATE * ((s1 - part.final[p, 0, rows]) + part.adj[p, 1, rows])
                field[p, S1, to] = new1
                field[p, RATE, to] = part.field[p, RATE, rows]
                gain[p, :, to] = part.gain[p, :, rows]
                old = foll[p, rows]
                new = old - STATE_RATE * ((old - part.final[p, 1, rows]) + came_lam[p])
                pull[p, 0, to] = pulls[p, 0, rows] + new1
                pull[p, 1, to] = pulls[p, 1, rows] + jnp.where(t < nt - 1, new, 0.0)

    far_at, beside_at, beside_from = jnp.where(low, EDGE, 0), jnp.where(low, 0, EDGE), jnp.where(low, ROWS - EDGE, 0)

    def to_rest(*fields):
        for p in range(2):
            for f in fields:
                field4[p, f, span(beside_at, EDGE)] = field3[p, f, span(beside_from, EDGE)]

    when(before[0], fin_copies[0].wait_recv)
    when(after[0], lam_copies[0].wait_recv)
    renew(one, pull1, back1, foll1, fin1, lam1, field3, gain3, pull3, 0)
    again.coefficients()
    when(before[0], fin_copies[1].wait_recv)
    when(after[0], lam_copies[1].wait_recv)
    renew(two, pull2, back2, foll2, fin2, lam2, field4, gain4, pull4, far_at)
    to_rest(S0, S1, RATE)
    for p in range(2):
        gain4[p, :, span(beside_at, EDGE)] = gain3[p, :, span(beside_from, EDGE)]
        pull4[p, :, span(beside_at, EDGE)] = pull3[p, :, span(beside_from, EDGE)]
        adj1[p, :, 0:ROWS] = pull3[p]
        adj2[p, :, 0:END] = pull4[p]
    rest.coefficients()

    def total(ref, rows):
        got = ref[0, rows]
        for i in range(1, ref.shape[0]):
            got = got + ref[i, rows]
        return got

    def new_bed(part, sums, field, start):
        groups = (part.rows - 16) // 8
        sides = total(sums, slice(8 * groups, 8 * groups + 8))
        for k in range(groups):
            rows, to = slice(8 + 8 * k, 16 + 8 * k), span(start + 8 * k, 8)
            main = total(sums, slice(8 * k, 8 * k + 8))
            side = jnp.where(within(at8, -8, 16), rolled(sides, -16 * k), 0.0)
            for p, got in enumerate((main, side)):
                field[p, BED, to] = part.field[p, BED, rows] - BED_RATE * got

    for copy, come in exchanged:
        when(come, copy.wait_recv)
    new_bed(one, pairs, field3, 0)

    split = ROWS - EDGE

    def descend(part, into, sums, count):
        part.slopes()
        for k in range(STEPS):
            part.forward(k)
        copy = remote(*after, part.final.at[0, 1, 8:8 + count], into)
        when(after[0], copy.start)
        part.force()
        part.pull()
        for r in range(0, count, BLOCK):
            sums[t, r:r + BLOCK] = part.bed_gradient(8 + r, BLOCK)[0]
        return copy, broadcast(sums)

    fin3_copy, sent3 = descend(again, fin3, sums3, split)
    for copy in sent2:
        copy.wait_recv()
    new_bed(two, sums2, field4, far_at)
    to_rest(BED)
    fin4_copy, sent4 = descend(rest, fin4, sums4, EDGE)

    out3, out4 = jnp.where(low, 0, EDGE), jnp.where(low, split, 0)
    both_passes = ((again, fin3, fin3_copy, sent3, sums3, split, out3), (rest, fin4, fin4_copy, sent4, sums4, EDGE, out4))
    for part, fin, copy, _, _, count, out in both_passes:
        when(before[0], copy.wait_recv)
        for r in range(0, count, BLOCK):
            rows, short, to = slice(8 + r, 8 + r + BLOCK), slice(r, r + BLOCK), span(out + r, BLOCK)
            begun = jnp.where(t == 0, ff[BACK, span(home + out + r, BLOCK)], fin[short])
            s0, s1 = part.field[0, S0, rows], part.field[0, S1, rows]
            states_out[0, to] = s0 - STATE_RATE * ((s0 - begun) + part.adj[0, 0, rows])
            states_out[1, to] = s1 - STATE_RATE * ((s1 - part.final[0, 0, rows]) + part.adj[0, 1, rows])
    for part, _, _, sent, sums, count, out in both_passes:
        for copy in sent:
            copy.wait_recv()
        for r in range(0, count, BLOCK):
            rows, short, to = slice(8 + r, 8 + r + BLOCK), slice(r, r + BLOCK), span(out + r, BLOCK)
            now = part.field[0, BED, rows]
            bed_out[to] = now - BED_RATE * (total(sums, short) + (now - ff[BED, span(home + out + r, BLOCK)]))
    for copy, to in copies:
        when(to, copy.wait_send)


def emit(states, bed, states_out, bed_out, sem):
    copies = [pltpu.make_async_copy(src, dst, sem.at[i]) for i, (src, dst) in enumerate(((states, states_out), (bed, bed_out)))]
    for copy in copies:
        copy.start()
    for copy in copies:
        copy.wait()


def solution(mesh):
    nt, nx, ny = (mesh.shape[a] for a in ("tm", "gx", "gy"))
    f32 = jnp.float32

    def vmem(*shape, dtype=f32):
        return pltpu.VMEM(shape, dtype)

    def model_scratch(rows):
        return [
            vmem(2, 4, rows + 8, COLS), vmem(2, 2, rows, COLS), vmem(2, 2, rows, COLS),
            vmem(STEPS - 1, 2, 2, rows + 8, COLS), vmem(2, 2, rows + 8, COLS), vmem(2, 2, 8 + rows, COLS),
            vmem(2, 2, 8 + rows, COLS), vmem(2, 2, rows, COLS), vmem(2, 2, rows, COLS),
        ]

    def step(states, bed, background, mask, rate, cells, values):
        obs = cells.shape[-1]
        count = 23 + 6 + 2 + 2 + 2 + 1 + 2 * (nt // 2 - 1) + 3 * (nt - 1)
        out = pl.pallas_call(
            functools.partial(kernel, nt, nx, ny),
            out_shape=(pltpu.VMEM(states.shape, f32), pltpu.VMEM(bed.shape, f32)),
            out_specs=(pl.BlockSpec(memory_space=pltpu.VMEM),) * 2,
            in_specs=[pl.BlockSpec(memory_space=pltpu.HBM)] * 7,
            scratch_shapes=[
                vmem(FIELDS, HIGH, COLS),
                vmem(ROWS, COLS), vmem(ROWS, COLS, dtype=jnp.int32),
                vmem(2, 1, 1, obs, dtype=jnp.int32), vmem(2, 1, 1, obs),
                vmem(2, 2, 1, 1, obs, dtype=jnp.int32), vmem(2, 2, 1, 1, obs),
                vmem(ROWS, COLS), vmem(ROWS, COLS), vmem(HIGH, COLS), vmem(HIGH, COLS),
                vmem(HIGH, COLS), vmem(2, 2, 8, COLS), vmem(2, 3, 8, COLS), vmem(2, MID, COLS), vmem(2, END, COLS),
                *model_scratch(MID), *model_scratch(END),
                vmem(2, 4, ROWS + 8, COLS), vmem(2, 2, ROWS, COLS), vmem(2, 2, ROWS, COLS),
                vmem(2, 4, END + 8, COLS), vmem(2, 2, END, COLS), vmem(2, 2, END, COLS),
                vmem(2, 2, MID, COLS), vmem(2, 2, END, COLS), vmem(2, 2, ROWS, COLS), vmem(2, 2, END, COLS),
                vmem(2, MID, COLS), vmem(2, END, COLS),
                vmem(ROWS + 8, COLS), vmem(ROWS + 8, COLS), vmem(nt // 2, ROWS + 8, COLS), vmem(nt, EDGE + 8, COLS),
                vmem(nt, ROWS - EDGE, COLS), vmem(nt, EDGE, COLS),
                vmem(ROWS + 8, COLS), vmem(EDGE + 8, COLS), vmem(ROWS + 8, COLS), vmem(EDGE + 8, COLS),
                vmem(ROWS - EDGE, COLS), vmem(EDGE, COLS),
                vmem(ROWS + 8, COLS), vmem(EDGE + 8, COLS), vmem(ROWS + 8, COLS), vmem(EDGE + 8, COLS),
                pltpu.SemaphoreType.DMA((7,)),
                pltpu.SemaphoreType.DMA((count,)), pltpu.SemaphoreType.DMA((count,)),
            ],
            compiler_params=pltpu.CompilerParams(
                collective_id=0, has_side_effects=True, vmem_limit_bytes=32 << 20),
            name="assimilate",
        )(*(pltpu.with_memory_space_constraint(x, pltpu.HBM)
            for x in (states, bed, background, mask, rate, cells, values)))
        return pl.pallas_call(
            emit,
            out_shape=(jax.ShapeDtypeStruct(states.shape, f32), jax.ShapeDtypeStruct(bed.shape, f32)),
            in_specs=[pl.BlockSpec(memory_space=pltpu.VMEM)] * 2,
            out_specs=(pl.BlockSpec(memory_space=pl.ANY),) * 2,
            scratch_shapes=[pltpu.SemaphoreType.DMA((2,))],
            compiler_params=pltpu.CompilerParams(vmem_limit_bytes=1 << 20),
            name="emit",
        )(*(pltpu.with_memory_space_constraint(x, pltpu.VMEM) for x in out))

    return jax.shard_map(
        step,
        mesh=mesh,
        in_specs=(P("tm", "gx", "gy"),) + (P("gx", "gy"),) * 4 + (P("tm", "gx", "gy", None),) * 2,
        out_specs=(P("tm", "gx", "gy"), P("gx", "gy")),
        check_vma=False,
    )
```

```python
import functools

import jax
import jax.numpy as jnp
from jax import lax
from jax.experimental import pallas as pl
from jax.experimental.pallas import tpu as pltpu
from jax.sharding import PartitionSpec as P

STEPS = 4
ROWS, COLS = 64, 128
EDGE = 16
HIGH = ROWS + 2 * EDGE
MID = ROWS + EDGE
END = 2 * EDGE
BLOCK = 16
BED_RATE = 0.1
STATE_RATE = 0.5
MESH = pl.DeviceIdType.MESH

BED, S0, S1, RATE, N0, N1, V0, V1, BACK = range(9)
FIELDS = 9
STRIP = ((0, 16), (16, 16), (32, 16), (48, 16), (64, 12), (76, 12), (88, 12), (100, 12), (112, 8))
CORNERS = ((1, -1), (1, 1), (-1, -1), (-1, 1))
AROUND = ((1, 0), (-1, 0)) + CORNERS + ((0, -1), (0, 1))


def when(cond, act):
    if cond is None:
        act()
    else:
        pl.when(cond)(act)


def span(start, size):
    return pl.ds(pl.multiple_of(start, 8), size)


def rolled(value, shift):
    shift %= COLS
    return value if shift == 0 else pltpu.roll(value, shift, value.ndim - 1)


def lane(shape):
    return lax.broadcasted_iota(jnp.int32, shape, len(shape) - 1)


def ahead(main, side):
    last = lane(main.shape) == COLS - 1
    main, side = rolled(main, -1), rolled(side, -1)
    return jnp.where(last, side, main), jnp.where(last, main, side)


def behind(main, side):
    first = lane(main.shape) == 0
    main, side = rolled(main, 1), rolled(side, 1)
    return jnp.where(first, side, main), jnp.where(first, main, side)


def within(at, start, width):
    start %= COLS
    if start + width <= COLS:
        return (at >= start) & (at < start + width)
    return (at >= start) | (at < start + width - COLS)


def counted(cell, value, rows, skip):
    obs = cell.shape[-1]
    row, col = cell // COLS - skip, cell % COLS
    in_row = (lax.broadcasted_iota(jnp.int32, (rows, obs), 0) == row).astype(jnp.float32)
    in_col = (lax.broadcasted_iota(jnp.int32, (COLS, obs), 0) == col).astype(jnp.float32).astype(jnp.bfloat16)
    parts = [in_row.astype(jnp.bfloat16)]
    rest = value
    for _ in range(3):
        part = rest.astype(jnp.bfloat16)
        rest = rest - part.astype(jnp.float32)
        parts.append((in_row * part.astype(jnp.float32)).astype(jnp.bfloat16))
    got = lax.dot_general(jnp.concatenate(parts, axis=0), in_col, (((1,), (1,)), ((), ())),
                          preferred_element_type=jnp.float32)
    return got[:rows], (got[3 * rows:] + got[2 * rows:3 * rows]) + got[rows:2 * rows]


class Model:
    def __init__(self, rows, field, coef, slope, path, kept, adj, flux, grad, gain, final):
        self.rows, self.field, self.coef, self.slope, self.path, self.kept = rows, field, coef, slope, path, kept
        self.adj, self.flux, self.grad, self.gain, self.final = adj, flux, grad, gain, final

    def blocks(self):
        return [slice(r, r + BLOCK) for r in range(0, self.rows, BLOCK)]

    def clear_ends(self):
        tail = slice(self.rows, self.rows + 8)
        for ref, index in ((self.field, (Ellipsis, tail, slice(None))), (self.path, (Ellipsis, tail, slice(None))),
                           (self.adj, (Ellipsis, tail, slice(None))), (self.flux, (Ellipsis, slice(0, 8), slice(None))),
                           (self.grad, (Ellipsis, slice(0, 8), slice(None)))):
            ref[index] = jnp.zeros_like(ref[index])

    def coefficients(self):
        def mean_rate(a, b):
            return jnp.where(jnp.minimum(a, b) > 0.0, 0.5 * (a + b), 0.0)

        for rows in self.blocks():
            both = [self.field[p, RATE, rows] for p in range(2)]
            for p, (here, up) in enumerate(zip(both, ahead(*both))):
                self.coef[1, p, rows] = mean_rate(here, up)
                self.coef[0, p, rows] = mean_rate(here, self.field[p, RATE, rows.start + 1:rows.stop + 1])

    def slopes(self):
        for rows in self.blocks():
            both = [self.field[p, BED, rows] for p in range(2)]
            for p, (here, up) in enumerate(zip(both, ahead(*both))):
                self.slope[1, p, rows] = up - here
                self.slope[0, p, rows] = self.field[p, BED, rows.start + 1:rows.stop + 1] - here

    def thick(self, k, p, rows):
        return self.field[p, S0:S1 + 1, rows] if k == 0 else self.path[k - 1, p, :, rows]

    def down(self, k, rows, here):
        up = [self.thick(k, p, slice(rows.start + 1, rows.stop + 1)) for p in range(2)]
        return [0.5 * (here[p] + up[p]) for p in range(2)], [(up[p] - here[p]) + self.slope[0, p, rows] for p in range(2)]

    def across(self, rows, here):
        up = ahead(*here)
        return [0.5 * (here[p] + up[p]) for p in range(2)], [(up[p] - here[p]) + self.slope[1, p, rows] for p in range(2)]

    def forward(self, k):
        for rows in self.blocks():
            here = [self.thick(k, p, rows) for p in range(2)]
            mean, step = zip(self.down(k, rows, here), self.across(rows, here))
            for p in range(2):
                self.kept[k, 0, p, :, rows], self.kept[k, 1, p, :, rows] = mean[1][p], step[1][p]
            f = [[self.coef[d, p, rows] * mean[d][p] * mean[d][p] * step[d][p] for p in range(2)] for d in range(2)]
            left = behind(*f[1])
            for p in range(2):
                self.flux[p, :, 8 + rows.start:8 + rows.stop] = f[0][p]
                new = here[p] + ((f[0][p] - self.flux[p, :, 7 + rows.start:7 + rows.stop]) + (f[1][p] - left[p]))
                if k + 1 < STEPS:
                    self.path[k, p, :, rows] = new
                else:
                    self.final[p, :, rows] = new

    def force(self):
        for rows in self.blocks():
            for p in range(2):
                self.adj[p, :, rows] = self.gain[p, :, rows] * self.final[p, :, rows] - self.adj[p, :, rows]

    def backward(self, k):
        for rows in self.blocks():
            down = self.down(k, rows, [self.thick(k, p, rows) for p in range(2)])
            mean, step = ([down[i], [self.kept[k, i, p, :, rows] for p in range(2)]] for i in range(2))
            lam = [self.adj[p, :, rows] for p in range(2)]
            up = [[self.adj[p, :, rows.start + 1:rows.stop + 1] for p in range(2)], ahead(*lam)]
            spot = slice(8 + rows.start, 8 + rows.stop)
            keep, give = [[], []], [[], []]
            for d in range(2):
                for p in range(2):
                    q = self.coef[d, p, rows] * mean[d][p] * (lam[p] - up[d][p])
                    g, e = q * mean[d][p], q * step[d][p]
                    keep[d].append(e - g)
                    give[d].append(e + g)
                    both = g[0] + g[1]
                    self.grad[d, p, spot] = both if k == STEPS - 1 else self.grad[d, p, spot] + both
            given = behind(*give[1])
            for p in range(2):
                self.flux[p, :, spot] = give[0][p]
                self.adj[p, :, rows] = (
                    lam[p] + (keep[0][p] + self.flux[p, :, 7 + rows.start:7 + rows.stop]) + (keep[1][p] + given[p]))

    def pull(self):
        for k in reversed(range(STEPS)):
            self.backward(k)

    def bed_gradient(self, r, count):
        spot, before = slice(8 + r, 8 + r + count), slice(7 + r, 7 + r + count)
        left = behind(self.grad[1, 0, spot], self.grad[1, 1, spot])
        return [(self.grad[0, p, before] - self.grad[0, p, spot]) + (left[p] - self.grad[1, p, spot]) for p in range(2)]


def kernel(
    nt, nx, ny,
    states, bed, background, mask, rate, cells, values,
    states_out, bed_out,
    ff, rate_in, mask_in, cell_in, value_in, cell_near, value_near, left_out, right_out, left_in, right_in,
    nxt, fold_out, fold_in, foll1, foll2,
    field1, coef1, slope1, path1, kept1, adj1, flux1, grad1, gain1, final1,
    field2, coef2, slope2, path2, kept2, adj2, flux2, grad2, gain2, final2,
    field3, gain3, final3, field4, gain4, final4,
    pull1, pull2, pull3, pull4, back1, back2,
    mine, theirs, pairs, sums2, sums3, sums4, fin_out1, fin_out2, fin1, fin2, fin3, fin4, lam_out1, lam_out2, lam1, lam2,
    load_sem, send_sem, recv_sem,
):
    t, gx, gy = lax.axis_index("tm"), lax.axis_index("gx"), lax.axis_index("gy")
    half = nx // 2
    low = gx < half
    high = jnp.logical_not(low)

    def place(side, is_low):
        return jnp.where(is_low, *{-1: (0, MID), 0: (EDGE, 0), 1: (MID, ROWS)}[side])

    home = place(0, low)
    inner = span(home, ROWS)

    loads = [
        pltpu.make_async_copy(src, dst, load_sem.at[i])
        for i, (src, dst) in enumerate((
            (cells, cell_in), (values, value_in), (mask, mask_in), (rate, rate_in),
            (states, ff.at[S0:S1 + 1, inner]), (bed, ff.at[BED, inner]), (background, ff.at[BACK, inner]),
        ))
    ]
    for load in loads:
        load.start()

    def near(dt, dx, dy):
        parts = [None if d == 0 else (pos + d >= 0) & (pos + d < size)
                 for d, pos, size in ((dt, t, nt), (dx, gx, nx), (dy, gy, ny))]
        parts = [p for p in parts if p is not None]
        return functools.reduce(jnp.logical_and, parts), (t + dt, gx + dx, gy + dy)

    def middle(dx):
        return low != (gx + dx < half)

    def both(*conds):
        conds = [c for c in conds if c is not None]
        return functools.reduce(jnp.logical_and, conds) if conds else None

    peers = []
    for dt in (0, -1, 1):
        for dx, dy in AROUND:
            cond, target = near(dt, dx, dy)
            peers.append((both(cond, jnp.logical_not(middle(dx))) if dt and dx else cond, target))
    peers += [(None, (lax.rem(t + d, nt), gx, gy)) for d in range(1, nt)]
    barrier = pltpu.get_barrier_semaphore()
    expected = jnp.int32(0)
    for cond, target in peers:
        when(cond, functools.partial(pl.semaphore_signal, barrier, inc=1, device_id=target, device_id_type=MESH))
        expected = expected + (1 if cond is None else cond.astype(jnp.int32))

    def clear(cond, *parts):
        def act():
            for ref, index in parts:
                ref[index] = jnp.zeros_like(ref[index])
        pl.when(cond)(act)

    side_rows = slice(None)
    for cond, rows, side in ((gx == 0, slice(0, EDGE), 0), (gx == nx - 1, slice(ROWS, MID), 1)):
        clear(cond, (ff, (side_rows, rows)), (left_in, rows), (right_in, rows), (nxt, rows),
              (fold_in, (slice(None), 2 * side)), (value_near, side))
        pl.when(cond)(functools.partial(
            cell_near.__setitem__, side, jnp.full(cell_near.shape[1:], -1, jnp.int32)))
    clear(gy == 0, (left_in, ...), (fold_in, 0))
    clear(gy == ny - 1, (right_in, ...), (fold_in, 1))
    clear(t == nt - 1, (nxt, ...), (fold_in, ...))

    one = Model(MID, field1, coef1, slope1, path1, kept1, adj1, flux1, grad1, gain1, final1)
    two = Model(END, field2, coef2, slope2, path2, kept2, adj2, flux2, grad2, gain2, final2)
    again = Model(ROWS, field3, coef1, slope1, path1, kept1, adj1, flux1, grad1, gain3, final3)
    rest = Model(END, field4, coef2, slope2, path2, kept2, adj2, flux2, grad2, gain4, final4)
    for part in (one, two, again, rest):
        part.clear_ends()

    loads[0].wait()
    loads[1].wait()
    for j in range(2):
        ff[N0 + j, inner], ff[V0 + j, inner] = counted(cell_in[j, 0], value_in[j, 0], ROWS, 0)
    loads[2].wait()
    loads[3].wait()
    ff[RATE, inner] = jnp.where(mask_in[...] != 0, rate_in[...], 0.0)
    for load in loads[4:]:
        load.wait()

    at = lane((BLOCK, COLS))
    at8 = lane((8, COLS))
    for r in range(0, ROWS, BLOCK):
        to_left = to_right = jnp.zeros((BLOCK, COLS), jnp.float32)
        for f, (start, width) in enumerate(STRIP):
            turned = rolled(ff[f, span(home + r, BLOCK)], start)
            to_left = jnp.where(within(at, start, width), turned, to_left)
            to_right = jnp.where(within(at, start - width, width), turned, to_right)
        left_out[r:r + BLOCK] = to_left
        right_out[r:r + BLOCK] = to_right

    def fold(to, field):
        to_left = to_right = jnp.zeros((8, COLS), jnp.float32)
        for k in range(ROWS // 8):
            turned = rolled(field[span(home + 8 * k, 8)], 16 * k)
            to_left = jnp.where(within(at8, 16 * k, 16), turned, to_left)
            to_right = jnp.where(within(at8, 16 * k - 16, 16), turned, to_right)
        fold_out[to, 0], fold_out[to, 1] = to_left, to_right

    fold(0, ff.at[S0])

    def first_row(dx):
        return ROWS - EDGE if dx > 0 else 0

    copies = []

    def remote(to, target, src, dst):
        i = len(copies)
        copy = pltpu.make_async_remote_copy(
            src_ref=src, dst_ref=dst, send_sem=send_sem.at[i], recv_sem=recv_sem.at[i],
            device_id=target, device_id_type=MESH)
        copies.append((copy, to))
        return copy

    def halo(dt, dx, dy, pick, also_to=None, also_from=None):
        to, target = near(dt, dx, dy)
        come, _ = near(-dt, -dx, -dy)
        to, come = both(to, also_to), both(come, also_from)
        count = EDGE if dx else ROWS
        land = span(place(-dx, gx + dx < half), count)
        return remote(to, target, *pick(span(home + first_row(dx), count), pl.ds(first_row(dx), count), land)), to, come, dx

    def strips(dy):
        out, into = (left_out, right_in) if dy < 0 else (right_out, left_in)
        return lambda own, tile, land: (out.at[tile], into.at[land])

    early = [halo(0, dx, 0, lambda own, tile, land: (ff.at[0:4, own], ff.at[0:4, land])) for dx in (1, -1)]
    early += [halo(0, dx, dy, strips(dy)) for dx, dy in CORNERS + ((0, -1), (0, 1))]
    late = []
    for dx in (1, -1):
        side = 0 if dx > 0 else 1
        late.append(halo(0, dx, 0, lambda own, tile, land: (cell_in, cell_near.at[side])))
        late.append(halo(0, dx, 0, lambda own, tile, land: (value_in, value_near.at[side])))
    def next_slice(i, field, dx, dy):
        if dy == 0:
            return lambda own, tile, land: (field.at[own], nxt.at[land])
        return lambda own, tile, land: (fold_out.at[i, 0 if dy < 0 else 1], fold_in.at[1 if dy < 0 else 0, 1 - dx])

    next_tile = halo(-1, 0, 0, next_slice(0, ff.at[S0], 0, 0))
    for dx, dy in AROUND:
        conds = [None] * 2 if dx == 0 else [jnp.logical_not(middle(d)) for d in (dx, -dx)]
        late.append(halo(-1, dx, dy, next_slice(0, ff.at[S0], dx, dy), *conds))
    for dx in (1, -1):
        late.append(halo(0, dx, 0, lambda own, tile, land: (ff.at[BACK, own], ff.at[BACK, land]), t == 0, t == 0))
    onward = [halo(0, dx, dy, next_slice(1, nxt, dx, dy), *(both(t < nt - 1, middle(d)) for d in (dx, -dx)))
              for dx, dy in AROUND if dx]

    pl.semaphore_wait(barrier, expected)
    for copy, to, _, _ in [next_tile] + early + late:
        when(to, copy.start)
    when(next_tile[2], next_tile[0].wait_recv)

    @pl.when((t < nt - 1) & (middle(1) | middle(-1)))
    def _():
        fold(1, nxt)

    for copy, to, _, _ in onward:
        when(to, copy.start)

    def arrive(group, far):
        for copy, _, come, dx in group:
            if dx:
                when(come & (low if (dx > 0) != far else high), copy.wait_recv)
            elif not far:
                when(come, copy.wait_recv)

    def unpacked(f, rows):
        start, width = STRIP[f]
        return jnp.where(at < width, rolled(right_in[rows], -start),
                         jnp.where(at >= COLS - width, rolled(left_in[rows], -start), 0.0))

    def take(part, r, rows):
        to = slice(r, r + BLOCK)
        for f in range(4):
            part.field[0, f, to] = ff[f, rows]
            part.field[1, f, to] = unpacked(f, rows)

    def unfolded(spots):
        out = []
        for pair in spots:
            which = jnp.where(low, pair[0][0], pair[1][0])
            left, right = fold_in[0, which], fold_in[1, which]
            got = [jnp.where(at8 < 16, rolled(right, -16 * k), jnp.where(at8 >= COLS - 16, rolled(left, -16 * k), 0.0))
                   for _, k in pair]
            out.append(jnp.where(low, *got))
        return jnp.concatenate(out, axis=0)

    more = (t < nt - 1).astype(jnp.float32)

    def demand(part, pulls, back, foll, r, rows, spots):
        to = slice(r, r + BLOCK)
        back[0, to], back[1, to] = ff[BACK, rows], unpacked(BACK, rows)
        for p in range(2):
            got = [ff[f, rows] if p == 0 else unpacked(f, rows) for f in (N0, N1, V0, V1)]
            following = nxt[rows] if p == 0 else unfolded(spots)
            foll[p, to] = following
            part.gain[p, 0, to], part.gain[p, 1, to] = got[0] + 1.0, got[1] + more
            pulls[p, 0, to], pulls[p, 1, to] = got[2], got[3]
            part.adj[p, 0, to] = got[2] + part.field[p, S1, to]
            part.adj[p, 1, to] = got[3] + following

    def beside(far):
        from_up = low if not far else high
        side, skip = jnp.where(from_up, 0, 1), jnp.where(from_up, ROWS - EDGE, 0)
        rows = span(MID if far else jnp.where(low, 0, ROWS), EDGE)
        for j in range(2):
            ff[N0 + j, rows], ff[V0 + j, rows] = counted(cell_near[side, j, 0], value_near[side, j, 0], EDGE, skip)

    arrive(early, False)
    for r in range(0, MID, BLOCK):
        take(one, r, slice(r, r + BLOCK))
    one.coefficients()
    one.slopes()
    for k in range(STEPS):
        one.forward(k)
    before, after = near(-1, 0, 0), near(1, 0, 0)

    def pack(to, groups, get):
        packed = jnp.zeros((8, COLS), jnp.float32)
        for k in range(groups):
            main, side = get(8 + 8 * k)
            to[8 * k:8 * k + 8] = main
            packed = jnp.where(within(at8, 16 * k - 8, 16), rolled(side, 16 * k), packed)
        to[8 * groups:8 * groups + 8] = packed

    def unpack(ref, groups, k):
        side = rolled(ref[8 * groups:8 * groups + 8], -16 * k)
        return ref[8 * k:8 * k + 8], jnp.where(within(at8, -8, 16), side, 0.0)

    def send_final(part, to, into):
        pack(to, (part.rows - 16) // 8, lambda r: [part.final[p, 1, r:r + 8] for p in range(2)])
        copy = remote(*after, to, into)
        when(after[0], copy.start)
        return copy

    def send_adjoint(part, to, into):
        pack(to, (part.rows - 16) // 8, lambda r: [part.adj[p, 0, r:r + 8] for p in range(2)])
        copy = remote(*before, to, into)
        when(before[0], copy.start)
        return copy

    fin_copies = [send_final(one, fin_out1, fin1)]
    arrive(late, False)
    beside(False)
    for r in range(0, MID, BLOCK):
        spots = []
        for g in (r // 8, r // 8 + 1):
            spots.append([(0, 6 + g) if g < 2 else (1, g - 2), (1, g) if g < 8 else (2, g - 8)])
        demand(one, pull1, back1, foll1, r, slice(r, r + BLOCK), spots)
    one.force()

    one.pull()

    def broadcast(buffer, in_order=False):
        out, base = [], len(copies)
        for d in sorted(range(1, nt), key=lambda d: d if in_order else -min(d, nt - d)):
            out.append(remote(None, (lax.rem(t + d, nt), gx, gy), buffer.at[t], buffer.at[t]))
        if not in_order:
            for copy in out:
                copy.start()
            return out
        for i in range(nt):
            spot = lax.rem(i + nt - t, nt) + base - 1

            @pl.when(t != i)
            def _():
                pltpu.make_async_remote_copy(
                    src_ref=buffer.at[t], dst_ref=buffer.at[t], send_sem=send_sem.at[spot], recv_sem=recv_sem.at[spot],
                    device_id=(i, gx, gy), device_id_type=MESH).start()
        return out

    def put_bed_gradient(part, buffer):
        pack(buffer.at[t], (part.rows - 16) // 8, lambda r: part.bed_gradient(r, 8))
        return broadcast(buffer)

    odd = lax.rem(t, 2)
    pack(mine, ROWS // 8, lambda r: one.bed_gradient(r, 8))
    to_partner = remote(None, (t + 1 - 2 * odd, gx, gy), mine, theirs)
    to_partner.start()

    spots2 = [[[(1, 6), (0, 6)], [(1, 7), (0, 7)]], [[(2, 0), (1, 0)], [(2, 1), (1, 1)]]]
    from2 = [span(jnp.where(low, ROWS, MID), BLOCK), span(jnp.where(low, MID, 0), BLOCK)]
    arrive(early, True)
    for i in range(2):
        take(two, BLOCK * i, from2[i])
    two.coefficients()
    two.slopes()
    for k in range(STEPS):
        two.forward(k)
    fin_copies.append(send_final(two, fin_out2, fin2))
    arrive(late, True)
    beside(True)
    arrive(onward, True)
    for i in range(2):
        demand(two, pull2, back2, foll2, BLOCK * i, from2[i], spots2[i])
    two.force()
    for k in (3, 2):
        two.backward(k)
    to_partner.wait_recv()
    pair = t // 2
    pairs[pair] = mine[...] + theirs[...]
    exchanged = []
    for far in range(nt // 2 - 1, 0, -1):
        for parity in range(2):
            off = min((2 * far - parity) % nt, (2 * far + 1 - parity) % nt, key=lambda o: min(o, nt - o))
            copy = remote(odd == (parity + off) % 2, (lax.rem(t + nt - off, nt), gx, gy), pairs.at[pair], pairs.at[pair])
            exchanged.append((copy, odd == parity))
            when(odd == (parity + off) % 2, copy.start)
    for k in (1, 0):
        two.backward(k)
    sent2 = put_bed_gradient(two, sums2)
    lam_copies = [send_adjoint(one, lam_out1, lam1), send_adjoint(two, lam_out2, lam2)]

    def renew(part, pulls, back, foll, fin, lam, field, gain, pull, start):
        groups = (part.rows - 16) // 8
        for k in range(groups):
            rows, to = slice(8 + 8 * k, 16 + 8 * k), span(start + 8 * k, 8)
            came, came_lam = unpack(fin, groups, k), unpack(lam, groups, k)
            for p in range(2):
                begun = jnp.where(t == 0, back[p, rows], came[p])
                s0, s1 = part.field[p, S0, rows], part.field[p, S1, rows]
                field[p, S0, to] = s0 - STATE_RATE * ((s0 - begun) + part.adj[p, 0, rows])
                new1 = s1 - STATE_RATE * ((s1 - part.final[p, 0, rows]) + part.adj[p, 1, rows])
                field[p, S1, to] = new1
                field[p, RATE, to] = part.field[p, RATE, rows]
                gain[p, :, to] = part.gain[p, :, rows]
                old = foll[p, rows]
                new = old - STATE_RATE * ((old - part.final[p, 1, rows]) + came_lam[p])
                pull[p, 0, to] = pulls[p, 0, rows] + new1
                pull[p, 1, to] = pulls[p, 1, rows] + jnp.where(t < nt - 1, new, 0.0)

    far_at, beside_at, beside_from = jnp.where(low, EDGE, 0), jnp.where(low, 0, EDGE), jnp.where(low, ROWS - EDGE, 0)

    def to_rest(*fields):
        for p in range(2):
            for f in fields:
                field4[p, f, span(beside_at, EDGE)] = field3[p, f, span(beside_from, EDGE)]

    when(before[0], fin_copies[0].wait_recv)
    when(after[0], lam_copies[0].wait_recv)
    renew(one, pull1, back1, foll1, fin1, lam1, field3, gain3, pull3, 0)
    again.coefficients()
    when(before[0], fin_copies[1].wait_recv)
    when(after[0], lam_copies[1].wait_recv)
    renew(two, pull2, back2, foll2, fin2, lam2, field4, gain4, pull4, far_at)
    to_rest(S0, S1, RATE)
    for p in range(2):
        gain4[p, :, span(beside_at, EDGE)] = gain3[p, :, span(beside_from, EDGE)]
        pull4[p, :, span(beside_at, EDGE)] = pull3[p, :, span(beside_from, EDGE)]
        adj1[p, :, 0:ROWS] = pull3[p]
        adj2[p, :, 0:END] = pull4[p]
    rest.coefficients()

    def total(ref, rows):
        got = ref[0, rows]
        for i in range(1, ref.shape[0]):
            got = got + ref[i, rows]
        return got

    def new_bed(part, sums, field, start):
        groups = (part.rows - 16) // 8
        sides = total(sums, slice(8 * groups, 8 * groups + 8))
        for k in range(groups):
            rows, to = slice(8 + 8 * k, 16 + 8 * k), span(start + 8 * k, 8)
            main = total(sums, slice(8 * k, 8 * k + 8))
            side = jnp.where(within(at8, -8, 16), rolled(sides, -16 * k), 0.0)
            for p, got in enumerate((main, side)):
                field[p, BED, to] = part.field[p, BED, rows] - BED_RATE * got

    for copy, come in exchanged:
        when(come, copy.wait_recv)
    new_bed(one, pairs, field3, 0)

    split = ROWS - EDGE

    def descend(part, into, sums, count):
        part.slopes()
        for k in range(STEPS):
            part.forward(k)
        copy = remote(*after, part.final.at[0, 1, 8:8 + count], into)
        when(after[0], copy.start)
        part.force()
        part.pull()
        for r in range(0, count, BLOCK):
            sums[t, r:r + BLOCK] = part.bed_gradient(8 + r, BLOCK)[0]
        return copy, broadcast(sums, True)

    fin3_copy, sent3 = descend(again, fin3, sums3, split)
    for copy in sent2:
        copy.wait_recv()
    new_bed(two, sums2, field4, far_at)
    to_rest(BED)
    fin4_copy, sent4 = descend(rest, fin4, sums4, EDGE)

    out3, out4 = jnp.where(low, 0, EDGE), jnp.where(low, split, 0)
    both_passes = ((again, fin3, fin3_copy, sent3, sums3, split, out3), (rest, fin4, fin4_copy, sent4, sums4, EDGE, out4))
    for part, fin, copy, _, _, count, out in both_passes:
        when(before[0], copy.wait_recv)
        for r in range(0, count, BLOCK):
            rows, short, to = slice(8 + r, 8 + r + BLOCK), slice(r, r + BLOCK), span(out + r, BLOCK)
            begun = jnp.where(t == 0, ff[BACK, span(home + out + r, BLOCK)], fin[short])
            s0, s1 = part.field[0, S0, rows], part.field[0, S1, rows]
            states_out[0, to] = s0 - STATE_RATE * ((s0 - begun) + part.adj[0, 0, rows])
            states_out[1, to] = s1 - STATE_RATE * ((s1 - part.final[0, 0, rows]) + part.adj[0, 1, rows])
    for part, _, _, sent, sums, count, out in both_passes:
        for copy in sent:
            copy.wait_recv()
        for r in range(0, count, BLOCK):
            rows, short, to = slice(8 + r, 8 + r + BLOCK), slice(r, r + BLOCK), span(out + r, BLOCK)
            now = part.field[0, BED, rows]
            bed_out[to] = now - BED_RATE * (total(sums, short) + (now - ff[BED, span(home + out + r, BLOCK)]))
    for copy, to in copies:
        when(to, copy.wait_send)


def emit(states, bed, states_out, bed_out, sem):
    copies = [pltpu.make_async_copy(src, dst, sem.at[i]) for i, (src, dst) in enumerate(((states, states_out), (bed, bed_out)))]
    for copy in copies:
        copy.start()
    for copy in copies:
        copy.wait()


def solution(mesh):
    nt, nx, ny = (mesh.shape[a] for a in ("tm", "gx", "gy"))
    f32 = jnp.float32

    def vmem(*shape, dtype=f32):
        return pltpu.VMEM(shape, dtype)

    def model_scratch(rows):
        return [
            vmem(2, 4, rows + 8, COLS), vmem(2, 2, rows, COLS), vmem(2, 2, rows, COLS),
            vmem(STEPS - 1, 2, 2, rows + 8, COLS), vmem(STEPS, 2, 2, 2, rows, COLS),
            vmem(2, 2, rows + 8, COLS), vmem(2, 2, 8 + rows, COLS),
            vmem(2, 2, 8 + rows, COLS), vmem(2, 2, rows, COLS), vmem(2, 2, rows, COLS),
        ]

    def step(states, bed, background, mask, rate, cells, values):
        obs = cells.shape[-1]
        count = 23 + 6 + 2 + 2 + 2 + 1 + 2 * (nt // 2 - 1) + 3 * (nt - 1)
        out = pl.pallas_call(
            functools.partial(kernel, nt, nx, ny),
            out_shape=(pltpu.VMEM(states.shape, f32), pltpu.VMEM(bed.shape, f32)),
            out_specs=(pl.BlockSpec(memory_space=pltpu.VMEM),) * 2,
            in_specs=[pl.BlockSpec(memory_space=pltpu.HBM)] * 7,
            scratch_shapes=[
                vmem(FIELDS, HIGH, COLS),
                vmem(ROWS, COLS), vmem(ROWS, COLS, dtype=jnp.int32),
                vmem(2, 1, 1, obs, dtype=jnp.int32), vmem(2, 1, 1, obs),
                vmem(2, 2, 1, 1, obs, dtype=jnp.int32), vmem(2, 2, 1, 1, obs),
                vmem(ROWS, COLS), vmem(ROWS, COLS), vmem(HIGH, COLS), vmem(HIGH, COLS),
                vmem(HIGH, COLS), vmem(2, 2, 8, COLS), vmem(2, 3, 8, COLS), vmem(2, MID, COLS), vmem(2, END, COLS),
                *model_scratch(MID), *model_scratch(END),
                vmem(2, 4, ROWS + 8, COLS), vmem(2, 2, ROWS, COLS), vmem(2, 2, ROWS, COLS),
                vmem(2, 4, END + 8, COLS), vmem(2, 2, END, COLS), vmem(2, 2, END, COLS),
                vmem(2, 2, MID, COLS), vmem(2, 2, END, COLS), vmem(2, 2, ROWS, COLS), vmem(2, 2, END, COLS),
                vmem(2, MID, COLS), vmem(2, END, COLS),
                vmem(ROWS + 8, COLS), vmem(ROWS + 8, COLS), vmem(nt // 2, ROWS + 8, COLS), vmem(nt, EDGE + 8, COLS),
                vmem(nt, ROWS - EDGE, COLS), vmem(nt, EDGE, COLS),
                vmem(ROWS + 8, COLS), vmem(EDGE + 8, COLS), vmem(ROWS + 8, COLS), vmem(EDGE + 8, COLS),
                vmem(ROWS - EDGE, COLS), vmem(EDGE, COLS),
                vmem(ROWS + 8, COLS), vmem(EDGE + 8, COLS), vmem(ROWS + 8, COLS), vmem(EDGE + 8, COLS),
                pltpu.SemaphoreType.DMA((7,)),
                pltpu.SemaphoreType.DMA((count,)), pltpu.SemaphoreType.DMA((count,)),
            ],
            compiler_params=pltpu.CompilerParams(
                collective_id=0, has_side_effects=True, vmem_limit_bytes=32 << 20),
            name="assimilate",
        )(*(pltpu.with_memory_space_constraint(x, pltpu.HBM)
            for x in (states, bed, background, mask, rate, cells, values)))
        return pl.pallas_call(
            emit,
            out_shape=(jax.ShapeDtypeStruct(states.shape, f32), jax.ShapeDtypeStruct(bed.shape, f32)),
            in_specs=[pl.BlockSpec(memory_space=pltpu.VMEM)] * 2,
            out_specs=(pl.BlockSpec(memory_space=pl.ANY),) * 2,
            scratch_shapes=[pltpu.SemaphoreType.DMA((2,))],
            compiler_params=pltpu.CompilerParams(vmem_limit_bytes=1 << 20),
            name="emit",
        )(*(pltpu.with_memory_space_constraint(x, pltpu.VMEM) for x in out))

    return jax.shard_map(
        step,
        mesh=mesh,
        in_specs=(P("tm", "gx", "gy"),) + (P("gx", "gy"),) * 4 + (P("tm", "gx", "gy", None),) * 2,
        out_specs=(P("tm", "gx", "gy"), P("gx", "gy")),
        check_vma=False,
    )
```

```python
import functools

import jax
import jax.numpy as jnp
from jax import lax
from jax.experimental import pallas as pl
from jax.experimental.pallas import tpu as pltpu
from jax.sharding import PartitionSpec as P

STEPS = 4
ROWS, COLS = 64, 128
EDGE = 16
HIGH = ROWS + 2 * EDGE
MID = ROWS + EDGE
END = 2 * EDGE
BLOCK = 16
BED_RATE = 0.1
STATE_RATE = 0.5
MESH = pl.DeviceIdType.MESH

BED, S0, S1, RATE, N0, N1, V0, V1, BACK = range(9)
FIELDS = 9
STRIP = ((0, 16), (16, 16), (32, 16), (48, 16), (64, 12), (76, 12), (88, 12), (100, 12), (112, 8))
CORNERS = ((1, -1), (1, 1), (-1, -1), (-1, 1))
AROUND = ((1, 0), (-1, 0)) + CORNERS + ((0, -1), (0, 1))


def when(cond, act):
    if cond is None:
        act()
    else:
        pl.when(cond)(act)


def span(start, size):
    return pl.ds(pl.multiple_of(start, 8), size)


def rolled(value, shift):
    shift %= COLS
    return value if shift == 0 else pltpu.roll(value, shift, value.ndim - 1)


def lane(shape):
    return lax.broadcasted_iota(jnp.int32, shape, len(shape) - 1)


def ahead(main, side):
    last = lane(main.shape) == COLS - 1
    main, side = rolled(main, -1), rolled(side, -1)
    return jnp.where(last, side, main), jnp.where(last, main, side)


def behind(main, side):
    first = lane(main.shape) == 0
    main, side = rolled(main, 1), rolled(side, 1)
    return jnp.where(first, side, main), jnp.where(first, main, side)


def within(at, start, width):
    start %= COLS
    if start + width <= COLS:
        return (at >= start) & (at < start + width)
    return (at >= start) | (at < start + width - COLS)


def counted(cell, value, rows, skip):
    obs = cell.shape[-1]
    row, col = cell // COLS - skip, cell % COLS
    in_row = (lax.broadcasted_iota(jnp.int32, (rows, obs), 0) == row).astype(jnp.float32)
    in_col = (lax.broadcasted_iota(jnp.int32, (COLS, obs), 0) == col).astype(jnp.float32).astype(jnp.bfloat16)
    parts = [in_row.astype(jnp.bfloat16)]
    rest = value
    for _ in range(3):
        part = rest.astype(jnp.bfloat16)
        rest = rest - part.astype(jnp.float32)
        parts.append((in_row * part.astype(jnp.float32)).astype(jnp.bfloat16))
    got = lax.dot_general(jnp.concatenate(parts, axis=0), in_col, (((1,), (1,)), ((), ())),
                          preferred_element_type=jnp.float32)
    return got[:rows], (got[3 * rows:] + got[2 * rows:3 * rows]) + got[rows:2 * rows]


class Model:
    def __init__(self, rows, field, coef, slope, path, kept, adj, flux, grad, gain, final):
        self.rows, self.field, self.coef, self.slope, self.path, self.kept = rows, field, coef, slope, path, kept
        self.adj, self.flux, self.grad, self.gain, self.final = adj, flux, grad, gain, final

    def blocks(self):
        return [slice(r, r + BLOCK) for r in range(0, self.rows, BLOCK)]

    def clear_ends(self):
        tail = slice(self.rows, self.rows + 8)
        for ref, index in ((self.field, (Ellipsis, tail, slice(None))), (self.path, (Ellipsis, tail, slice(None))),
                           (self.adj, (Ellipsis, tail, slice(None))), (self.flux, (Ellipsis, slice(0, 8), slice(None))),
                           (self.grad, (Ellipsis, slice(0, 8), slice(None)))):
            ref[index] = jnp.zeros_like(ref[index])

    def coefficients(self):
        def mean_rate(a, b):
            return jnp.where(jnp.minimum(a, b) > 0.0, 0.5 * (a + b), 0.0)

        for rows in self.blocks():
            both = [self.field[p, RATE, rows] for p in range(2)]
            for p, (here, up) in enumerate(zip(both, ahead(*both))):
                self.coef[1, p, rows] = mean_rate(here, up)
                self.coef[0, p, rows] = mean_rate(here, self.field[p, RATE, rows.start + 1:rows.stop + 1])

    def slopes(self):
        for rows in self.blocks():
            both = [self.field[p, BED, rows] for p in range(2)]
            for p, (here, up) in enumerate(zip(both, ahead(*both))):
                self.slope[1, p, rows] = up - here
                self.slope[0, p, rows] = self.field[p, BED, rows.start + 1:rows.stop + 1] - here

    def thick(self, k, p, rows):
        return self.field[p, S0:S1 + 1, rows] if k == 0 else self.path[k - 1, p, :, rows]

    def down(self, k, rows, here):
        up = [self.thick(k, p, slice(rows.start + 1, rows.stop + 1)) for p in range(2)]
        return [0.5 * (here[p] + up[p]) for p in range(2)], [(up[p] - here[p]) + self.slope[0, p, rows] for p in range(2)]

    def across(self, rows, here):
        up = ahead(*here)
        return [0.5 * (here[p] + up[p]) for p in range(2)], [(up[p] - here[p]) + self.slope[1, p, rows] for p in range(2)]

    def forward(self, k):
        for rows in self.blocks():
            here = [self.thick(k, p, rows) for p in range(2)]
            mean, step = zip(self.down(k, rows, here), self.across(rows, here))
            for p in range(2):
                self.kept[k, 0, p, :, rows], self.kept[k, 1, p, :, rows] = mean[1][p], step[1][p]
            f = [[self.coef[d, p, rows] * mean[d][p] * mean[d][p] * step[d][p] for p in range(2)] for d in range(2)]
            left = behind(*f[1])
            for p in range(2):
                self.flux[p, :, 8 + rows.start:8 + rows.stop] = f[0][p]
                new = here[p] + ((f[0][p] - self.flux[p, :, 7 + rows.start:7 + rows.stop]) + (f[1][p] - left[p]))
                if k + 1 < STEPS:
                    self.path[k, p, :, rows] = new
                else:
                    self.final[p, :, rows] = new

    def force(self):
        for rows in self.blocks():
            for p in range(2):
                self.adj[p, :, rows] = self.gain[p, :, rows] * self.final[p, :, rows] - self.adj[p, :, rows]

    def backward(self, k):
        for rows in self.blocks():
            down = self.down(k, rows, [self.thick(k, p, rows) for p in range(2)])
            mean, step = ([down[i], [self.kept[k, i, p, :, rows] for p in range(2)]] for i in range(2))
            lam = [self.adj[p, :, rows] for p in range(2)]
            up = [[self.adj[p, :, rows.start + 1:rows.stop + 1] for p in range(2)], ahead(*lam)]
            spot = slice(8 + rows.start, 8 + rows.stop)
            keep, give = [[], []], [[], []]
            for d in range(2):
                for p in range(2):
                    q = self.coef[d, p, rows] * mean[d][p] * (lam[p] - up[d][p])
                    g, e = q * mean[d][p], q * step[d][p]
                    keep[d].append(e - g)
                    give[d].append(e + g)
                    both = g[0] + g[1]
                    self.grad[d, p, spot] = both if k == STEPS - 1 else self.grad[d, p, spot] + both
            given = behind(*give[1])
            for p in range(2):
                self.flux[p, :, spot] = give[0][p]
                self.adj[p, :, rows] = (
                    lam[p] + (keep[0][p] + self.flux[p, :, 7 + rows.start:7 + rows.stop]) + (keep[1][p] + given[p]))

    def pull(self):
        for k in reversed(range(STEPS)):
            self.backward(k)

    def bed_gradient(self, r, count):
        spot, before = slice(8 + r, 8 + r + count), slice(7 + r, 7 + r + count)
        left = behind(self.grad[1, 0, spot], self.grad[1, 1, spot])
        return [(self.grad[0, p, before] - self.grad[0, p, spot]) + (left[p] - self.grad[1, p, spot]) for p in range(2)]


def kernel(
    nt, nx, ny,
    states, bed, background, mask, rate, cells, values,
    states_out, bed_out,
    ff, rate_in, mask_in, cell_in, value_in, cell_near, value_near, left_out, right_out, left_in, right_in,
    nxt, fold_out, fold_in, foll1, foll2,
    field1, coef1, slope1, path1, kept1, adj1, flux1, grad1, gain1, final1,
    field2, coef2, slope2, path2, kept2, adj2, flux2, grad2, gain2, final2,
    field3, gain3, final3, field4, gain4, final4,
    pull1, pull2, pull3, pull4, back1, back2,
    mine, theirs, pairs, sums2, sums3, sums4, fin_out1, fin_out2, fin1, fin2, fin3, fin4, lam_out1, lam_out2, lam1, lam2,
    load_sem, send_sem, recv_sem,
):
    t, gx, gy = lax.axis_index("tm"), lax.axis_index("gx"), lax.axis_index("gy")
    half = nx // 2
    low = gx < half
    high = jnp.logical_not(low)

    def place(side, is_low):
        return jnp.where(is_low, *{-1: (0, MID), 0: (EDGE, 0), 1: (MID, ROWS)}[side])

    home = place(0, low)
    inner = span(home, ROWS)

    loads = [
        pltpu.make_async_copy(src, dst, load_sem.at[i])
        for i, (src, dst) in enumerate((
            (cells, cell_in), (values, value_in), (mask, mask_in), (rate, rate_in),
            (states, ff.at[S0:S1 + 1, inner]), (bed, ff.at[BED, inner]), (background, ff.at[BACK, inner]),
        ))
    ]
    for load in loads:
        load.start()

    def near(dt, dx, dy):
        parts = [None if d == 0 else (pos + d >= 0) & (pos + d < size)
                 for d, pos, size in ((dt, t, nt), (dx, gx, nx), (dy, gy, ny))]
        parts = [p for p in parts if p is not None]
        return functools.reduce(jnp.logical_and, parts), (t + dt, gx + dx, gy + dy)

    def middle(dx):
        return low != (gx + dx < half)

    def both(*conds):
        conds = [c for c in conds if c is not None]
        return functools.reduce(jnp.logical_and, conds) if conds else None

    peers = []
    for dt in (0, -1, 1):
        for dx, dy in AROUND:
            cond, target = near(dt, dx, dy)
            peers.append((both(cond, jnp.logical_not(middle(dx))) if dt and dx else cond, target))
    peers += [(None, (lax.rem(t + d, nt), gx, gy)) for d in range(1, nt)]
    barrier = pltpu.get_barrier_semaphore()
    expected = jnp.int32(0)
    for cond, target in peers:
        when(cond, functools.partial(pl.semaphore_signal, barrier, inc=1, device_id=target, device_id_type=MESH))
        expected = expected + (1 if cond is None else cond.astype(jnp.int32))

    def clear(cond, *parts):
        def act():
            for ref, index in parts:
                ref[index] = jnp.zeros_like(ref[index])
        pl.when(cond)(act)

    side_rows = slice(None)
    for cond, rows, side in ((gx == 0, slice(0, EDGE), 0), (gx == nx - 1, slice(ROWS, MID), 1)):
        clear(cond, (ff, (side_rows, rows)), (left_in, rows), (right_in, rows), (nxt, rows),
              (fold_in, (slice(None), 2 * side)), (value_near, side))
        pl.when(cond)(functools.partial(
            cell_near.__setitem__, side, jnp.full(cell_near.shape[1:], -1, jnp.int32)))
    clear(gy == 0, (left_in, ...), (fold_in, 0))
    clear(gy == ny - 1, (right_in, ...), (fold_in, 1))
    clear(t == nt - 1, (nxt, ...), (fold_in, ...))

    one = Model(MID, field1, coef1, slope1, path1, kept1, adj1, flux1, grad1, gain1, final1)
    two = Model(END, field2, coef2, slope2, path2, kept2, adj2, flux2, grad2, gain2, final2)
    again = Model(ROWS, field3, coef1, slope1, path1, kept1, adj1, flux1, grad1, gain3, final3)
    rest = Model(END, field4, coef2, slope2, path2, kept2, adj2, flux2, grad2, gain4, final4)
    for part in (one, two, again, rest):
        part.clear_ends()

    loads[0].wait()
    loads[1].wait()
    for j in range(2):
        ff[N0 + j, inner], ff[V0 + j, inner] = counted(cell_in[j, 0], value_in[j, 0], ROWS, 0)
    loads[2].wait()
    loads[3].wait()
    ff[RATE, inner] = jnp.where(mask_in[...] != 0, rate_in[...], 0.0)
    for load in loads[4:]:
        load.wait()

    at = lane((BLOCK, COLS))
    at8 = lane((8, COLS))
    for r in range(0, ROWS, BLOCK):
        to_left = to_right = jnp.zeros((BLOCK, COLS), jnp.float32)
        for f, (start, width) in enumerate(STRIP):
            turned = rolled(ff[f, span(home + r, BLOCK)], start)
            to_left = jnp.where(within(at, start, width), turned, to_left)
            to_right = jnp.where(within(at, start - width, width), turned, to_right)
        left_out[r:r + BLOCK] = to_left
        right_out[r:r + BLOCK] = to_right

    def fold(to, field):
        to_left = to_right = jnp.zeros((8, COLS), jnp.float32)
        for k in range(ROWS // 8):
            turned = rolled(field[span(home + 8 * k, 8)], 16 * k)
            to_left = jnp.where(within(at8, 16 * k, 16), turned, to_left)
            to_right = jnp.where(within(at8, 16 * k - 16, 16), turned, to_right)
        fold_out[to, 0], fold_out[to, 1] = to_left, to_right

    fold(0, ff.at[S0])

    def first_row(dx):
        return ROWS - EDGE if dx > 0 else 0

    copies = []

    def remote(to, target, src, dst):
        i = len(copies)
        copy = pltpu.make_async_remote_copy(
            src_ref=src, dst_ref=dst, send_sem=send_sem.at[i], recv_sem=recv_sem.at[i],
            device_id=target, device_id_type=MESH)
        copies.append((copy, to))
        return copy

    def halo(dt, dx, dy, pick, also_to=None, also_from=None):
        to, target = near(dt, dx, dy)
        come, _ = near(-dt, -dx, -dy)
        to, come = both(to, also_to), both(come, also_from)
        count = EDGE if dx else ROWS
        land = span(place(-dx, gx + dx < half), count)
        return remote(to, target, *pick(span(home + first_row(dx), count), pl.ds(first_row(dx), count), land)), to, come, dx

    def strips(dy):
        out, into = (left_out, right_in) if dy < 0 else (right_out, left_in)
        return lambda own, tile, land: (out.at[tile], into.at[land])

    early = [halo(0, dx, 0, lambda own, tile, land: (ff.at[0:4, own], ff.at[0:4, land])) for dx in (1, -1)]
    early += [halo(0, dx, dy, strips(dy)) for dx, dy in CORNERS + ((0, -1), (0, 1))]
    late = []
    for dx in (1, -1):
        side = 0 if dx > 0 else 1
        late.append(halo(0, dx, 0, lambda own, tile, land: (cell_in, cell_near.at[side])))
        late.append(halo(0, dx, 0, lambda own, tile, land: (value_in, value_near.at[side])))
    def next_slice(i, field, dx, dy):
        if dy == 0:
            return lambda own, tile, land: (field.at[own], nxt.at[land])
        return lambda own, tile, land: (fold_out.at[i, 0 if dy < 0 else 1], fold_in.at[1 if dy < 0 else 0, 1 - dx])

    next_tile = halo(-1, 0, 0, next_slice(0, ff.at[S0], 0, 0))
    for dx, dy in AROUND:
        conds = [None] * 2 if dx == 0 else [jnp.logical_not(middle(d)) for d in (dx, -dx)]
        late.append(halo(-1, dx, dy, next_slice(0, ff.at[S0], dx, dy), *conds))
    for dx in (1, -1):
        late.append(halo(0, dx, 0, lambda own, tile, land: (ff.at[BACK, own], ff.at[BACK, land]), t == 0, t == 0))
    onward = [halo(0, dx, dy, next_slice(1, nxt, dx, dy), *(both(t < nt - 1, middle(d)) for d in (dx, -dx)))
              for dx, dy in AROUND if dx]

    pl.semaphore_wait(barrier, expected)
    for copy, to, _, _ in [next_tile] + early + late:
        when(to, copy.start)
    when(next_tile[2], next_tile[0].wait_recv)

    @pl.when((t < nt - 1) & (middle(1) | middle(-1)))
    def _():
        fold(1, nxt)

    for copy, to, _, _ in onward:
        when(to, copy.start)

    def arrive(group, far):
        for copy, _, come, dx in group:
            if dx:
                when(come & (low if (dx > 0) != far else high), copy.wait_recv)
            elif not far:
                when(come, copy.wait_recv)

    def unpacked(f, rows):
        start, width = STRIP[f]
        return jnp.where(at < width, rolled(right_in[rows], -start),
                         jnp.where(at >= COLS - width, rolled(left_in[rows], -start), 0.0))

    def take(part, r, rows):
        to = slice(r, r + BLOCK)
        for f in range(4):
            part.field[0, f, to] = ff[f, rows]
            part.field[1, f, to] = unpacked(f, rows)

    def unfolded(spots):
        out = []
        for pair in spots:
            which = jnp.where(low, pair[0][0], pair[1][0])
            left, right = fold_in[0, which], fold_in[1, which]
            got = [jnp.where(at8 < 16, rolled(right, -16 * k), jnp.where(at8 >= COLS - 16, rolled(left, -16 * k), 0.0))
                   for _, k in pair]
            out.append(jnp.where(low, *got))
        return jnp.concatenate(out, axis=0)

    more = (t < nt - 1).astype(jnp.float32)

    def demand(part, pulls, back, foll, r, rows, spots):
        to = slice(r, r + BLOCK)
        back[0, to], back[1, to] = ff[BACK, rows], unpacked(BACK, rows)
        for p in range(2):
            got = [ff[f, rows] if p == 0 else unpacked(f, rows) for f in (N0, N1, V0, V1)]
            following = nxt[rows] if p == 0 else unfolded(spots)
            foll[p, to] = following
            part.gain[p, 0, to], part.gain[p, 1, to] = got[0] + 1.0, got[1] + more
            pulls[p, 0, to], pulls[p, 1, to] = got[2], got[3]
            part.adj[p, 0, to] = got[2] + part.field[p, S1, to]
            part.adj[p, 1, to] = got[3] + following

    def beside(far):
        from_up = low if not far else high
        side, skip = jnp.where(from_up, 0, 1), jnp.where(from_up, ROWS - EDGE, 0)
        rows = span(MID if far else jnp.where(low, 0, ROWS), EDGE)
        for j in range(2):
            ff[N0 + j, rows], ff[V0 + j, rows] = counted(cell_near[side, j, 0], value_near[side, j, 0], EDGE, skip)

    arrive(early, False)
    for r in range(0, MID, BLOCK):
        take(one, r, slice(r, r + BLOCK))
    one.coefficients()
    one.slopes()
    for k in range(STEPS):
        one.forward(k)
    before, after = near(-1, 0, 0), near(1, 0, 0)

    def pack(to, groups, get):
        packed = jnp.zeros((8, COLS), jnp.float32)
        for k in range(groups):
            main, side = get(8 + 8 * k)
            to[8 * k:8 * k + 8] = main
            packed = jnp.where(within(at8, 16 * k - 8, 16), rolled(side, 16 * k), packed)
        to[8 * groups:8 * groups + 8] = packed

    def unpack(ref, groups, k):
        side = rolled(ref[8 * groups:8 * groups + 8], -16 * k)
        return ref[8 * k:8 * k + 8], jnp.where(within(at8, -8, 16), side, 0.0)

    def send_final(part, to, into):
        pack(to, (part.rows - 16) // 8, lambda r: [part.final[p, 1, r:r + 8] for p in range(2)])
        copy = remote(*after, to, into)
        when(after[0], copy.start)
        return copy

    def send_adjoint(part, to, into):
        pack(to, (part.rows - 16) // 8, lambda r: [part.adj[p, 0, r:r + 8] for p in range(2)])
        copy = remote(*before, to, into)
        when(before[0], copy.start)
        return copy

    fin_copies = [send_final(one, fin_out1, fin1)]
    arrive(late, False)
    beside(False)
    for r in range(0, MID, BLOCK):
        spots = []
        for g in (r // 8, r // 8 + 1):
            spots.append([(0, 6 + g) if g < 2 else (1, g - 2), (1, g) if g < 8 else (2, g - 8)])
        demand(one, pull1, back1, foll1, r, slice(r, r + BLOCK), spots)
    one.force()

    one.pull()

    def broadcast(buffer, in_order=False):
        out, base = [], len(copies)
        for d in sorted(range(1, nt), key=lambda d: d if in_order else -min(d, nt - d)):
            out.append(remote(None, (lax.rem(t + d, nt), gx, gy), buffer.at[t], buffer.at[t]))
        if not in_order:
            for copy in out:
                copy.start()
            return out
        def begin(targets):
            for i in targets:
                spot = lax.rem(i + nt - t, nt) + base - 1

                @pl.when(t != i)
                def _():
                    pltpu.make_async_remote_copy(
                        src_ref=buffer.at[t], dst_ref=buffer.at[t], send_sem=send_sem.at[spot], recv_sem=recv_sem.at[spot],
                        device_id=(i, gx, gy), device_id_type=MESH).start()

        begin(range(nt // 2))
        return out, functools.partial(begin, range(nt // 2, nt))

    def put_bed_gradient(part, buffer):
        pack(buffer.at[t], (part.rows - 16) // 8, lambda r: part.bed_gradient(r, 8))
        return broadcast(buffer)

    odd = lax.rem(t, 2)
    pack(mine, ROWS // 8, lambda r: one.bed_gradient(r, 8))
    to_partner = remote(None, (t + 1 - 2 * odd, gx, gy), mine, theirs)
    to_partner.start()

    spots2 = [[[(1, 6), (0, 6)], [(1, 7), (0, 7)]], [[(2, 0), (1, 0)], [(2, 1), (1, 1)]]]
    from2 = [span(jnp.where(low, ROWS, MID), BLOCK), span(jnp.where(low, MID, 0), BLOCK)]
    arrive(early, True)
    for i in range(2):
        take(two, BLOCK * i, from2[i])
    two.coefficients()
    two.slopes()
    for k in range(STEPS):
        two.forward(k)
    fin_copies.append(send_final(two, fin_out2, fin2))
    arrive(late, True)
    beside(True)
    arrive(onward, True)
    for i in range(2):
        demand(two, pull2, back2, foll2, BLOCK * i, from2[i], spots2[i])
    two.force()
    for k in (3, 2):
        two.backward(k)
    to_partner.wait_recv()
    pair = t // 2
    pairs[pair] = mine[...] + theirs[...]
    exchanged = []
    for far in range(nt // 2 - 1, 0, -1):
        for parity in range(2):
            off = min((2 * far - parity) % nt, (2 * far + 1 - parity) % nt, key=lambda o: min(o, nt - o))
            copy = remote(odd == (parity + off) % 2, (lax.rem(t + nt - off, nt), gx, gy), pairs.at[pair], pairs.at[pair])
            exchanged.append((copy, odd == parity))
            when(odd == (parity + off) % 2, copy.start)
    for k in (1, 0):
        two.backward(k)
    sent2 = put_bed_gradient(two, sums2)
    lam_copies = [send_adjoint(one, lam_out1, lam1), send_adjoint(two, lam_out2, lam2)]

    def renew(part, pulls, back, foll, fin, lam, field, gain, pull, start):
        groups = (part.rows - 16) // 8
        for k in range(groups):
            rows, to = slice(8 + 8 * k, 16 + 8 * k), span(start + 8 * k, 8)
            came, came_lam = unpack(fin, groups, k), unpack(lam, groups, k)
            for p in range(2):
                begun = jnp.where(t == 0, back[p, rows], came[p])
                s0, s1 = part.field[p, S0, rows], part.field[p, S1, rows]
                field[p, S0, to] = s0 - STATE_RATE * ((s0 - begun) + part.adj[p, 0, rows])
                new1 = s1 - STATE_RATE * ((s1 - part.final[p, 0, rows]) + part.adj[p, 1, rows])
                field[p, S1, to] = new1
                field[p, RATE, to] = part.field[p, RATE, rows]
                gain[p, :, to] = part.gain[p, :, rows]
                old = foll[p, rows]
                new = old - STATE_RATE * ((old - part.final[p, 1, rows]) + came_lam[p])
                pull[p, 0, to] = pulls[p, 0, rows] + new1
                pull[p, 1, to] = pulls[p, 1, rows] + jnp.where(t < nt - 1, new, 0.0)

    far_at, beside_at, beside_from = jnp.where(low, EDGE, 0), jnp.where(low, 0, EDGE), jnp.where(low, ROWS - EDGE, 0)

    def to_rest(*fields):
        for p in range(2):
            for f in fields:
                field4[p, f, span(beside_at, EDGE)] = field3[p, f, span(beside_from, EDGE)]

    when(before[0], fin_copies[0].wait_recv)
    when(after[0], lam_copies[0].wait_recv)
    renew(one, pull1, back1, foll1, fin1, lam1, field3, gain3, pull3, 0)
    again.coefficients()
    when(before[0], fin_copies[1].wait_recv)
    when(after[0], lam_copies[1].wait_recv)
    renew(two, pull2, back2, foll2, fin2, lam2, field4, gain4, pull4, far_at)
    to_rest(S0, S1, RATE)
    for p in range(2):
        gain4[p, :, span(beside_at, EDGE)] = gain3[p, :, span(beside_from, EDGE)]
        pull4[p, :, span(beside_at, EDGE)] = pull3[p, :, span(beside_from, EDGE)]
        adj1[p, :, 0:ROWS] = pull3[p]
        adj2[p, :, 0:END] = pull4[p]
    rest.coefficients()

    def total(ref, rows):
        got = ref[0, rows]
        for i in range(1, ref.shape[0]):
            got = got + ref[i, rows]
        return got

    def new_bed(part, sums, field, start):
        groups = (part.rows - 16) // 8
        sides = total(sums, slice(8 * groups, 8 * groups + 8))
        for k in range(groups):
            rows, to = slice(8 + 8 * k, 16 + 8 * k), span(start + 8 * k, 8)
            main = total(sums, slice(8 * k, 8 * k + 8))
            side = jnp.where(within(at8, -8, 16), rolled(sides, -16 * k), 0.0)
            for p, got in enumerate((main, side)):
                field[p, BED, to] = part.field[p, BED, rows] - BED_RATE * got

    for copy, come in exchanged:
        when(come, copy.wait_recv)
    new_bed(one, pairs, field3, 0)

    split = ROWS - EDGE

    def descend(part, into, sums, count):
        part.slopes()
        for k in range(STEPS):
            part.forward(k)
        copy = remote(*after, part.final.at[0, 1, 8:8 + count], into)
        when(after[0], copy.start)
        part.force()
        part.pull()
        for r in range(0, count, BLOCK):
            sums[t, r:r + BLOCK] = part.bed_gradient(8 + r, BLOCK)[0]
        return copy, broadcast(sums, True)

    fin3_copy, (sent3, begin3) = descend(again, fin3, sums3, split)
    for copy in sent2:
        copy.wait_recv()
    new_bed(two, sums2, field4, far_at)
    to_rest(BED)
    fin4_copy, (sent4, begin4) = descend(rest, fin4, sums4, EDGE)
    begin3()
    begin4()

    out3, out4 = jnp.where(low, 0, EDGE), jnp.where(low, split, 0)
    both_passes = ((again, fin3, fin3_copy, sent3, sums3, split, out3), (rest, fin4, fin4_copy, sent4, sums4, EDGE, out4))
    for part, fin, copy, _, _, count, out in both_passes:
        when(before[0], copy.wait_recv)
        for r in range(0, count, BLOCK):
            rows, short, to = slice(8 + r, 8 + r + BLOCK), slice(r, r + BLOCK), span(out + r, BLOCK)
            begun = jnp.where(t == 0, ff[BACK, span(home + out + r, BLOCK)], fin[short])
            s0, s1 = part.field[0, S0, rows], part.field[0, S1, rows]
            states_out[0, to] = s0 - STATE_RATE * ((s0 - begun) + part.adj[0, 0, rows])
            states_out[1, to] = s1 - STATE_RATE * ((s1 - part.final[0, 0, rows]) + part.adj[0, 1, rows])
    for part, _, _, sent, sums, count, out in both_passes:
        for copy in sent:
            copy.wait_recv()
        for r in range(0, count, BLOCK):
            rows, short, to = slice(8 + r, 8 + r + BLOCK), slice(r, r + BLOCK), span(out + r, BLOCK)
            now = part.field[0, BED, rows]
            bed_out[to] = now - BED_RATE * (total(sums, short) + (now - ff[BED, span(home + out + r, BLOCK)]))
    for copy, to in copies:
        when(to, copy.wait_send)


def emit(states, bed, states_out, bed_out, sem):
    copies = [pltpu.make_async_copy(src, dst, sem.at[i]) for i, (src, dst) in enumerate(((states, states_out), (bed, bed_out)))]
    for copy in copies:
        copy.start()
    for copy in copies:
        copy.wait()


def solution(mesh):
    nt, nx, ny = (mesh.shape[a] for a in ("tm", "gx", "gy"))
    f32 = jnp.float32

    def vmem(*shape, dtype=f32):
        return pltpu.VMEM(shape, dtype)

    def model_scratch(rows):
        return [
            vmem(2, 4, rows + 8, COLS), vmem(2, 2, rows, COLS), vmem(2, 2, rows, COLS),
            vmem(STEPS - 1, 2, 2, rows + 8, COLS), vmem(STEPS, 2, 2, 2, rows, COLS),
            vmem(2, 2, rows + 8, COLS), vmem(2, 2, 8 + rows, COLS),
            vmem(2, 2, 8 + rows, COLS), vmem(2, 2, rows, COLS), vmem(2, 2, rows, COLS),
        ]

    def step(states, bed, background, mask, rate, cells, values):
        obs = cells.shape[-1]
        count = 23 + 6 + 2 + 2 + 2 + 1 + 2 * (nt // 2 - 1) + 3 * (nt - 1)
        out = pl.pallas_call(
            functools.partial(kernel, nt, nx, ny),
            out_shape=(pltpu.VMEM(states.shape, f32), pltpu.VMEM(bed.shape, f32)),
            out_specs=(pl.BlockSpec(memory_space=pltpu.VMEM),) * 2,
            in_specs=[pl.BlockSpec(memory_space=pltpu.HBM)] * 7,
            scratch_shapes=[
                vmem(FIELDS, HIGH, COLS),
                vmem(ROWS, COLS), vmem(ROWS, COLS, dtype=jnp.int32),
                vmem(2, 1, 1, obs, dtype=jnp.int32), vmem(2, 1, 1, obs),
                vmem(2, 2, 1, 1, obs, dtype=jnp.int32), vmem(2, 2, 1, 1, obs),
                vmem(ROWS, COLS), vmem(ROWS, COLS), vmem(HIGH, COLS), vmem(HIGH, COLS),
                vmem(HIGH, COLS), vmem(2, 2, 8, COLS), vmem(2, 3, 8, COLS), vmem(2, MID, COLS), vmem(2, END, COLS),
                *model_scratch(MID), *model_scratch(END),
                vmem(2, 4, ROWS + 8, COLS), vmem(2, 2, ROWS, COLS), vmem(2, 2, ROWS, COLS),
                vmem(2, 4, END + 8, COLS), vmem(2, 2, END, COLS), vmem(2, 2, END, COLS),
                vmem(2, 2, MID, COLS), vmem(2, 2, END, COLS), vmem(2, 2, ROWS, COLS), vmem(2, 2, END, COLS),
                vmem(2, MID, COLS), vmem(2, END, COLS),
                vmem(ROWS + 8, COLS), vmem(ROWS + 8, COLS), vmem(nt // 2, ROWS + 8, COLS), vmem(nt, EDGE + 8, COLS),
                vmem(nt, ROWS - EDGE, COLS), vmem(nt, EDGE, COLS),
                vmem(ROWS + 8, COLS), vmem(EDGE + 8, COLS), vmem(ROWS + 8, COLS), vmem(EDGE + 8, COLS),
                vmem(ROWS - EDGE, COLS), vmem(EDGE, COLS),
                vmem(ROWS + 8, COLS), vmem(EDGE + 8, COLS), vmem(ROWS + 8, COLS), vmem(EDGE + 8, COLS),
                pltpu.SemaphoreType.DMA((7,)),
                pltpu.SemaphoreType.DMA((count,)), pltpu.SemaphoreType.DMA((count,)),
            ],
            compiler_params=pltpu.CompilerParams(
                collective_id=0, has_side_effects=True, vmem_limit_bytes=32 << 20),
            name="assimilate",
        )(*(pltpu.with_memory_space_constraint(x, pltpu.HBM)
            for x in (states, bed, background, mask, rate, cells, values)))
        return pl.pallas_call(
            emit,
            out_shape=(jax.ShapeDtypeStruct(states.shape, f32), jax.ShapeDtypeStruct(bed.shape, f32)),
            in_specs=[pl.BlockSpec(memory_space=pltpu.VMEM)] * 2,
            out_specs=(pl.BlockSpec(memory_space=pl.ANY),) * 2,
            scratch_shapes=[pltpu.SemaphoreType.DMA((2,))],
            compiler_params=pltpu.CompilerParams(vmem_limit_bytes=1 << 20),
            name="emit",
        )(*(pltpu.with_memory_space_constraint(x, pltpu.VMEM) for x in out))

    return jax.shard_map(
        step,
        mesh=mesh,
        in_specs=(P("tm", "gx", "gy"),) + (P("gx", "gy"),) * 4 + (P("tm", "gx", "gy", None),) * 2,
        out_specs=(P("tm", "gx", "gy"), P("gx", "gy")),
        check_vma=False,
    )
```
